32 devices in a mesh: span: 4 (over y, x), seq: 2 (over core), mp: 4 (over z).
Axes of the slice: x: 2, y: 2, z: 4, core: 2. Of those that a mesh axis runs over, the one named last changes fastest.
Arguments:
- queries: bfloat16 [4, 128, 6144], P('span', 'seq', 'mp'), may hold values from -30 to 30
- keys: bfloat16 [4, 128, 1024], P('span', 'seq'), may hold values from -30 to 30
- values: bfloat16 [4, 128, 1024], P('span', 'seq'), may hold values from -6 to 6
- clip_ids: int32 [128], P('seq'), may hold values from 0 to 5, never falling along the last dimension, each value on 1 to 64 neighbouring positions
- block_mask: int32 [4, 4], replicated, may hold values from 0 to 1, as said below
- out_weight: bfloat16 [6144, 6144], P('mp'), may hold values from -0.078125 to 0.078125
Outputs:
- projected: bfloat16 [4, 128, 6144], P('span', 'seq', 'mp')
The draws below stay inside these ranges and needn't reach their ends.
Inputs may be any that keep to these rules, and one draw needn't show every extreme that they name: block_mask[c][c] is 1; block_mask[c][c2] is 0 unless c - 3 < c2 <= c. `clip_ids`: clip ids never fall along the rows; each clip has 1 to 64 rows, one exactly that many.
All inputs are finite; a program needn't handle non-finite values.
Results may differ from the reference program's by a relative error of at most 0.017.
Values may be sent and summed in bfloat16 or wider, within the bound.
A program may use at most 64 MiB of HBM per device.

```python
import math
import jax
import jax.numpy as jnp
import numpy as np
from jax import lax

D = 6144
HEADS = 48
HEAD_DIM = 128
WINDOW = 3
CLIPS = 6
GROUP = 6
KVD = 1024
NCHUNK = 4
ROWS = 128


def drawn_pair(key):
    key_queries, key_keys = jax.random.split(jax.random.fold_in(key, 11), 2)
    query_draw = jnp.clip(jax.random.normal(key_queries, (NCHUNK, ROWS, D), jnp.float32), -6.0, 6.0)
    key_draw = jnp.clip(jax.random.normal(key_keys, (NCHUNK, ROWS, KVD), jnp.float32), -6.0, 6.0)
    return (query_draw, key_draw)


def draw_queries(key, part):
    return drawn_pair(key)[0].astype(jnp.bfloat16)


def draw_keys(key, part):
    return drawn_pair(key)[1].astype(jnp.bfloat16)


def draw_block_mask(key, part):
    later = jnp.arange(NCHUNK)[:, None]
    earlier = jnp.arange(NCHUNK)[None, :]
    offset = later - earlier
    coins = jax.random.randint(jax.random.fold_in(key, 23), (NCHUNK, NCHUNK), 0, 2)
    inside = (offset >= 1) & (offset < WINDOW)
    return jnp.where(offset == 0, 1, jnp.where(inside, coins, 0)).astype(jnp.int32)


def shard_levels(stream_key, dims, shards, least, largest):
    level = 1.0
    for axis_at, shards_of in shards:
        steps = jax.random.uniform(jax.random.fold_in(jax.random.fold_in(stream_key, 6), axis_at), (shards_of,), jnp.float32, least / len(shards), largest / len(shards))
        level = level * jnp.repeat(jnp.exp(steps), dims[axis_at] // shards_of).reshape((-1,) + (1,) * (len(dims) - 1 - axis_at))
    return level


def profile(number_of, total, bound, skew):
    portions = [(1 << 20) // math.isqrt(standing ** skew) + 1 for standing in range(2, number_of + 1)]
    surplus, holding = total - bound - (number_of - 1), [1] * (number_of - 1)
    while surplus > 0:
        movable = [i for i in range(number_of - 1) if holding[i] < bound]
        pool, left = sum([portions[i] for i in movable]), surplus
        for i in movable:
            extra = min(bound - holding[i], max(1, left * portions[i] // pool), surplus)
            holding[i] = holding[i] + extra
            surplus = surplus - extra
    return np.array([bound] + holding)


def ragged_sizes(rng, amount, total, limit, skew):
    if amount == 2:
        one = jax.random.randint(rng, (), max(1, total - limit), min(limit, total - 1) + 1)
        return jnp.stack([one, total - one])
    lengths = jnp.asarray(profile(amount, total, limit, skew), jnp.int32)
    pairs = (amount - 1) // 2
    donor, receiver = lengths[1:1 + 2 * pairs:2], lengths[2:2 + 2 * pairs:2]
    room = jnp.minimum(donor - 1, limit - receiver)
    passed = jax.random.randint(jax.random.fold_in(rng, 1), (pairs,), 0, 1 << 20) % (room + 1)
    lengths = lengths.at[1:1 + 2 * pairs:2].set(donor - passed).at[2:2 + 2 * pairs:2].set(receiver + passed)
    return lengths[jax.random.permutation(jax.random.fold_in(rng, 2), amount)]


def noise(stream_key, shape, scale, reach, cuts=(), held_as=jnp.bfloat16):
    level = shard_levels(stream_key, shape, cuts, -0.22, 0.18) if cuts else 1.0
    result = jax.random.normal(stream_key, shape, jnp.float32) * scale * level
    return jnp.minimum(jnp.maximum(result, -reach), reach).astype(held_as)


def setup_inputs(seed: int = 0) -> dict:
    arg_keys = jax.random.split(jax.random.key(seed), 7)
    return {
        "queries": draw_queries(jax.random.fold_in(arg_keys[6], 71), 0),
        "keys": draw_keys(jax.random.fold_in(arg_keys[6], 71), 0),
        "values": noise(arg_keys[2], (NCHUNK, ROWS, KVD), 1.0, 6.0, ((0, 4), (1, 2))),
        "clip_ids": jnp.searchsorted(jnp.cumsum(ragged_sizes(arg_keys[3], CLIPS, ROWS, ROWS // 2, 2)), jnp.arange(ROWS), side="right").astype(jnp.int32),
        "block_mask": draw_block_mask(jax.random.fold_in(arg_keys[6], 71), 0),
        "out_weight": noise(arg_keys[5], (D, D), D ** -0.5, 0.078125, ((0, 4),)),
    }


def reference(queries, keys, values, clip_ids, block_mask, out_weight):
    score_scale = HEAD_DIM ** -0.5
    padding = WINDOW - 1
    padded_keys = jnp.concatenate([jnp.zeros((padding, ROWS, KVD), jnp.bfloat16), keys], axis=0)
    padded_values = jnp.concatenate([jnp.zeros((padding, ROWS, KVD), jnp.bfloat16), values], axis=0)
    padded_mask = jnp.concatenate([jnp.zeros((NCHUNK, padding), jnp.int32), block_mask], axis=1)
    same_clip = clip_ids[:, None] == clip_ids[None, :]

    def one_span(span_index):
        window_keys = lax.dynamic_slice_in_dim(padded_keys, span_index, WINDOW, 0).reshape(WINDOW * ROWS, KVD)
        window_values = lax.dynamic_slice_in_dim(padded_values, span_index, WINDOW, 0).reshape(WINDOW * ROWS, KVD)
        mask_row = lax.dynamic_index_in_dim(padded_mask, span_index, 0, keepdims=False)
        visible = lax.dynamic_slice_in_dim(mask_row, span_index, WINDOW, 0)
        allowed = (visible[:, None, None] == 1) & same_clip[None, :, :]
        allowed = jnp.transpose(allowed, (1, 0, 2)).reshape(ROWS, WINDOW * ROWS)
        span_queries = lax.dynamic_index_in_dim(queries, span_index, 0, keepdims=False)

        def head_out(head):
            start = (head * HEAD_DIM).astype(jnp.int32)
            kv_start = ((head // GROUP) * HEAD_DIM).astype(jnp.int32)
            query_head = lax.dynamic_slice_in_dim(span_queries, start, HEAD_DIM, 1)
            key_head = lax.dynamic_slice_in_dim(window_keys, kv_start, HEAD_DIM, 1)
            value_head = lax.dynamic_slice_in_dim(window_values, kv_start, HEAD_DIM, 1)
            s = jnp.dot(query_head, key_head.T, preferred_element_type=jnp.float32) * score_scale
            s = jnp.where(allowed, s, -jnp.inf)
            top = jnp.max(s, axis=1, keepdims=True)
            p = jnp.exp(s - top)
            total = jnp.sum(p, axis=1, keepdims=True)
            return jnp.dot(p.astype(jnp.bfloat16), value_head, preferred_element_type=jnp.float32) / total

        per_head = lax.map(head_out, jnp.arange(HEADS, dtype=jnp.int32))
        attended = jnp.transpose(per_head, (1, 0, 2)).reshape(ROWS, D).astype(jnp.bfloat16)
        return jnp.dot(attended, out_weight, preferred_element_type=jnp.float32).astype(jnp.bfloat16)

    return lax.map(one_span, jnp.arange(NCHUNK, dtype=jnp.int32))
```

```python
import functools
import jax
import jax.numpy as jnp
from jax import lax
from jax.experimental import pallas as pl
from jax.experimental.pallas import tpu as pltpu
from jax.sharding import PartitionSpec as P

HEAD_DIM = 128
WINDOW = 3
GROUP = 6
MASKED = -1e30
MESH = pl.DeviceIdType.MESH


def kernel(
    spans, seqs, n, pieces, kv_count, kv_total,
    q_ref, k_ref, v_ref, clip_ref, mask_ref, w_ref, out_ref,
    qbuf, kbuf, vbuf, own_clip, clips, wbuf, att, part, sendbuf, recvbuf, outbuf,
    local_sem, w_sem, span_send, seq_send, kv_recv, clip_send, clip_recv, sum_send, sum_recv, out_sem,
):
    rows, local_width = qbuf.shape
    head_count = local_width // HEAD_DIM
    width = wbuf.shape[2]
    chunk = width * pieces
    kv_width = kv_count * HEAD_DIM
    steps = n * pieces
    c = lax.axis_index("span")
    s = lax.axis_index("seq")
    me = lax.axis_index("mp")

    first_kv = jnp.minimum(me * head_count // GROUP, kv_total - kv_count)
    kv_columns = pl.ds(pl.multiple_of(first_kv * HEAD_DIM, HEAD_DIM), kv_width)

    local = [
        pltpu.make_async_copy(k_ref.at[0, :, kv_columns], kbuf.at[0, s], local_sem.at[0]),
        pltpu.make_async_copy(v_ref.at[0, :, kv_columns], vbuf.at[0, s], local_sem.at[1]),
        pltpu.make_async_copy(clip_ref, own_clip, local_sem.at[2]),
        pltpu.make_async_copy(q_ref.at[0], qbuf, local_sem.at[3]),
    ]
    for copy in local:
        copy.start()

    turn = 2 * (2 * me // n) - 1

    def chunk_at(step):
        return lax.rem(me + turn * (step + 1) + 2 * n, n)

    def w_copy(i):
        start = chunk_at(i // pieces) * chunk + lax.rem(i, pieces) * width
        return pltpu.make_async_copy(
            w_ref.at[:, pl.ds(pl.multiple_of(start, HEAD_DIM), width)], wbuf.at[i], w_sem.at[i]
        )

    barrier = pltpu.get_barrier_semaphore()
    for j in range(1, WINDOW):
        @pl.when(c >= j)
        def _():
            pl.semaphore_signal(barrier, inc=1, device_id={"span": c - j}, device_id_type=MESH)
    for d in range(1, seqs):
        pl.semaphore_signal(
            barrier, inc=1, device_id={"seq": lax.rem(s + d, seqs)}, device_id_type=MESH
        )

    @pl.when(me > 0)
    def _():
        pl.semaphore_signal(barrier, inc=1, device_id={"mp": me - 1}, device_id_type=MESH)

    @pl.when(me < n - 1)
    def _():
        pl.semaphore_signal(barrier, inc=1, device_id={"mp": me + 1}, device_id_type=MESH)

    def start_w(i, carry):
        w_copy(i).start()
        return carry

    lax.fori_loop(0, steps, start_w, 0)

    for j in range(1, WINDOW):
        @pl.when(c < j)
        def _():
            kbuf[j] = jnp.zeros(kbuf.shape[1:], kbuf.dtype)
            vbuf[j] = jnp.zeros(vbuf.shape[1:], vbuf.dtype)

    local[2].wait()
    clips[s] = jnp.broadcast_to(own_clip[...], clips.shape[1:])
    local[0].wait()
    local[1].wait()
    later_spans = jnp.minimum(spans - 1 - c, WINDOW - 1)
    z_neighbours = jnp.minimum(me, 1) + jnp.minimum(n - 1 - me, 1)
    pl.semaphore_wait(barrier, seqs - 1 + later_spans + z_neighbours)

    bufs = (kbuf, vbuf)

    def to_span(j, a):
        return pltpu.make_async_remote_copy(
            src_ref=bufs[a].at[0, s],
            dst_ref=bufs[a].at[j, s],
            send_sem=span_send.at[j, a],
            recv_sem=kv_recv.at[j, s, a],
            device_id={"span": c + j},
            device_id_type=MESH,
        )

    def to_seq(j, d, a):
        return pltpu.make_async_remote_copy(
            src_ref=bufs[a].at[j, s],
            dst_ref=bufs[a].at[j, s],
            send_sem=seq_send.at[j, d, a],
            recv_sem=kv_recv.at[j, s, a],
            device_id={"seq": lax.rem(s + d, seqs)},
            device_id_type=MESH,
        )

    def arrival(j, s2, a):
        return pltpu.make_async_remote_copy(
            src_ref=bufs[a].at[j, s2],
            dst_ref=bufs[a].at[j, s2],
            send_sem=seq_send.at[0, 0, a],
            recv_sem=kv_recv.at[j, s2, a],
            device_id={"seq": s2},
            device_id_type=MESH,
        )

    def clip_copy(d, source):
        return pltpu.make_async_remote_copy(
            src_ref=clips.at[source],
            dst_ref=clips.at[source],
            send_sem=clip_send.at[d],
            recv_sem=clip_recv.at[source],
            device_id={"seq": lax.rem(s + d, seqs)},
            device_id_type=MESH,
        )

    for a in range(2):
        for j in range(WINDOW - 1, 0, -1):
            @pl.when(c + j < spans)
            def _():
                to_span(j, a).start()
    for d in range(1, seqs):
        clip_copy(d, s).start()
    for a in range(2):
        for d in range(1, seqs):
            to_seq(0, d, a).start()

    def relay(a):
        for j in range(1, WINDOW):
            @pl.when(c >= j)
            def _():
                arrival(j, s, a).wait_recv()
                for d in range(1, seqs):
                    to_seq(j, d, a).start()

    def await_others(a):
        for d in range(1, seqs):
            arrival(0, lax.rem(s + d, seqs), a).wait_recv()
        for j in range(1, WINDOW):
            @pl.when(c >= j)
            def _():
                for d in range(1, seqs):
                    arrival(j, lax.rem(s + d, seqs), a).wait_recv()

    for d in range(1, seqs):
        clip_copy(d, lax.rem(s + d, seqs)).wait_recv()
    own = jnp.broadcast_to(own_clip[...], (rows, rows)).astype(jnp.float32)
    own_column = own.T
    same = [
        jnp.broadcast_to(clips[s2, 0:1, :], (rows, rows)).astype(jnp.float32) == own_column
        for s2 in range(seqs)
    ]
    blocks = []
    for j in range(WINDOW):
        entry = mask_ref[c, jnp.maximum(c - j, 0)]
        seen = jnp.where((c >= j) & (entry == 1), 0.0, MASKED).astype(jnp.float32)
        for s2 in range(seqs):
            blocks.append(jnp.where(same[s2], seen, MASKED))
    bias = jnp.concatenate(blocks, axis=1)

    local[3].wait()
    relay(0)
    relay(1)
    await_others(0)

    scale = HEAD_DIM ** (-0.5)
    key_count = WINDOW * seqs * rows
    stacked = GROUP if head_count % GROUP == 0 else 1
    probabilities = []
    for h in range(0, head_count, stacked):
        if head_count % GROUP == 0:
            g = h // GROUP
            keys = kbuf[:, :, :, g * HEAD_DIM:(g + 1) * HEAD_DIM]
        else:
            at = (me * head_count + h) // GROUP - first_kv
            keys = kbuf[:, :, :, 0:HEAD_DIM]
            for g in range(1, kv_count):
                keys = jnp.where(at == g, kbuf[:, :, :, g * HEAD_DIM:(g + 1) * HEAD_DIM], keys)
        keys = keys.reshape(key_count, HEAD_DIM)
        q = jnp.concatenate(
            [qbuf[:, i * HEAD_DIM:(i + 1) * HEAD_DIM] for i in range(h, h + stacked)], axis=0
        )
        scores = lax.dot_general(
            q, keys, (((1,), (1,)), ((), ())), preferred_element_type=jnp.float32
        ) * scale
        scores = scores.reshape(stacked, rows, key_count) + bias[None]
        top = jnp.max(scores, axis=2, keepdims=True)
        p = jnp.exp(scores - top)
        total = jnp.sum(p, axis=2, keepdims=True)
        probabilities.append((
            p.astype(jnp.bfloat16).reshape(stacked * rows, key_count),
            total.reshape(stacked * rows, 1),
        ))
    await_others(1)
    for h, (p, total) in zip(range(0, head_count, stacked), probabilities):
        if head_count % GROUP == 0:
            g = h // GROUP
            values = vbuf[:, :, :, g * HEAD_DIM:(g + 1) * HEAD_DIM]
        else:
            at = (me * head_count + h) // GROUP - first_kv
            values = vbuf[:, :, :, 0:HEAD_DIM]
            for g in range(1, kv_count):
                values = jnp.where(at == g, vbuf[:, :, :, g * HEAD_DIM:(g + 1) * HEAD_DIM], values)
        values = values.reshape(key_count, HEAD_DIM)
        o = jnp.dot(p, values, preferred_element_type=jnp.float32) / total
        o = o.astype(jnp.bfloat16)
        for i in range(stacked):
            att[:, (h + i) * HEAD_DIM:(h + i + 1) * HEAD_DIM] = o[i * rows:(i + 1) * rows]

    def pass_on(way, at):
        return pltpu.make_async_remote_copy(
            src_ref=sendbuf.at[at],
            dst_ref=recvbuf.at[way, at],
            send_sem=sum_send.at[at],
            recv_sem=sum_recv.at[way, at],
            device_id={"mp": me + 1 - 2 * way},
            device_id_type=MESH,
        )

    def project(i, carry):
        to = chunk_at(i // pieces)
        at = to * pieces + lax.rem(i, pieces)
        w_copy(i).wait()
        product = jnp.dot(att[...], wbuf[i], preferred_element_type=jnp.float32)
        part[at] = product

        @pl.when((me == 0) & (to > 0))
        def _():
            sendbuf[at] = product.astype(sendbuf.dtype)
            pass_on(0, at).start()

        @pl.when((me == n - 1) & (to < n - 1))
        def _():
            sendbuf[at] = product.astype(sendbuf.dtype)
            pass_on(1, at).start()

        return carry

    lax.fori_loop(0, steps, project, 0)

    def relay_sums(i, carry):
        up = (n - 1 - i // pieces) * pieces + lax.rem(i, pieces)

        @pl.when((me > 0) & (n - 1 - i // pieces > me))
        def _():
            pass_on(0, up).wait_recv()
            sendbuf[up] = (part[up] + recvbuf[0, up].astype(jnp.float32)).astype(sendbuf.dtype)
            pass_on(0, up).start()

        @pl.when((me < n - 1) & (i // pieces < me))
        def _():
            pass_on(1, i).wait_recv()
            sendbuf[i] = (part[i] + recvbuf[1, i].astype(jnp.float32)).astype(sendbuf.dtype)
            pass_on(1, i).start()

        return carry

    lax.fori_loop(0, (n - 2) * pieces, relay_sums, 0)

    def out_copy(i):
        return pltpu.make_async_copy(
            outbuf.at[i], out_ref.at[0, :, pl.ds(i * width, width)], out_sem.at[i]
        )

    for i in range(pieces):
        at = me * pieces + i

        @pl.when(me > 0)
        def _():
            pass_on(0, at).wait_recv()
            part[at] += recvbuf[0, at].astype(jnp.float32)

        @pl.when(me < n - 1)
        def _():
            pass_on(1, at).wait_recv()
            part[at] += recvbuf[1, at].astype(jnp.float32)

        outbuf[i] = part[at].astype(outbuf.dtype)
        out_copy(i).start()

    for a in range(2):
        for j in range(1, WINDOW):
            @pl.when(c + j < spans)
            def _():
                to_span(j, a).wait_send()
            @pl.when(c >= j)
            def _():
                for d in range(1, seqs):
                    to_seq(j, d, a).wait_send()
        for d in range(1, seqs):
            to_seq(0, d, a).wait_send()
    for d in range(1, seqs):
        clip_copy(d, s).wait_send()

    def sent(i, carry):
        @pl.when(i // pieces != me)
        def _():
            pass_on(0, i).wait_send()

        return carry

    lax.fori_loop(0, steps, sent, 0)
    for i in range(pieces):
        out_copy(i).wait()


def on_device(queries, keys, values, clip_ids, block_mask, out_weight):
    spans = lax.axis_size("span")
    seqs = lax.axis_size("seq")
    n = lax.axis_size("mp")
    _, rows, local_width = queries.shape
    head_count = local_width // HEAD_DIM
    kv_total = keys.shape[2] // HEAD_DIM
    firsts = [m * head_count // GROUP for m in range(n)]
    lasts = [((m + 1) * head_count - 1) // GROUP for m in range(n)]
    kv_count = max(b - a + 1 for a, b in zip(firsts, lasts))
    kv_width = kv_count * HEAD_DIM
    depth, out_width = out_weight.shape
    chunk = out_width // n
    width = 512 if chunk % 512 == 0 else HEAD_DIM
    pieces = chunk // width
    bf16 = jnp.bfloat16
    hbm = pl.BlockSpec(memory_space=pl.ANY)
    return pl.pallas_call(
        functools.partial(kernel, spans, seqs, n, pieces, kv_count, kv_total),
        out_shape=jax.ShapeDtypeStruct((1, rows, chunk), bf16),
        in_specs=[hbm, hbm, hbm, hbm, pl.BlockSpec(memory_space=pltpu.SMEM), hbm],
        out_specs=hbm,
        scratch_shapes=[
            pltpu.VMEM((rows, local_width), bf16),
            pltpu.VMEM((WINDOW, seqs, rows, kv_width), bf16),
            pltpu.VMEM((WINDOW, seqs, rows, kv_width), bf16),
            pltpu.VMEM((1, rows), jnp.int32),
            pltpu.VMEM((seqs, 8, rows), jnp.int32),
            pltpu.VMEM((n * pieces, depth, width), bf16),
            pltpu.VMEM((rows, local_width), bf16),
            pltpu.VMEM((n * pieces, rows, width), jnp.float32),
            pltpu.VMEM((n * pieces, rows, width), bf16),
            pltpu.VMEM((2, n * pieces, rows, width), bf16),
            pltpu.VMEM((pieces, rows, width), bf16),
            pltpu.SemaphoreType.DMA((4,)),
            pltpu.SemaphoreType.DMA((n * pieces,)),
            pltpu.SemaphoreType.DMA((WINDOW, 2)),
            pltpu.SemaphoreType.DMA((WINDOW, seqs, 2)),
            pltpu.SemaphoreType.DMA((WINDOW, seqs, 2)),
            pltpu.SemaphoreType.DMA((seqs,)),
            pltpu.SemaphoreType.DMA((seqs,)),
            pltpu.SemaphoreType.DMA((n * pieces,)),
            pltpu.SemaphoreType.DMA((2, n * pieces)),
            pltpu.SemaphoreType.DMA((pieces,)),
        ],
        compiler_params=pltpu.CompilerParams(
            collective_id=0, has_side_effects=True, vmem_limit_bytes=48 * 1024 * 1024
        ),
    )(queries, keys, values, clip_ids.reshape(1, rows), block_mask, out_weight)


def solution(mesh):
    in_specs = (
        P("span", "seq", "mp"),
        P("span", "seq", None),
        P("span", "seq", None),
        P("seq"),
        P(),
        P("mp", None),
    )
    out_specs = P("span", "seq", "mp")
    return jax.shard_map(
        on_device, mesh=mesh, in_specs=in_specs, out_specs=out_specs, check_vma=False
    )
```

```python
import functools
import jax
import jax.numpy as jnp
from jax import lax
from jax.experimental import pallas as pl
from jax.experimental.pallas import tpu as pltpu
from jax.sharding import PartitionSpec as P

HEAD_DIM = 128
WINDOW = 3
GROUP = 6
MASKED = -1e30
MESH = pl.DeviceIdType.MESH


def kernel(
    spans, seqs, n, pieces, kv_count, kv_total,
    q_ref, k_ref, v_ref, clip_ref, mask_ref, w_ref, out_ref,
    qbuf, kbuf, vbuf, own_clip, clips, wbuf, att, part, sendbuf, recvbuf, outbuf,
    local_sem, w_sem, span_send, seq_send, kv_recv, clip_send, clip_recv, sum_send, sum_recv, out_sem,
):
    rows, local_width = qbuf.shape
    head_count = local_width // HEAD_DIM
    width = wbuf.shape[2]
    chunk = width * pieces
    kv_width = kv_count * HEAD_DIM
    steps = n * pieces
    c = lax.axis_index("span")
    s = lax.axis_index("seq")
    me = lax.axis_index("mp")

    first_kv = jnp.minimum(me * head_count // GROUP, kv_total - kv_count)
    kv_columns = pl.ds(pl.multiple_of(first_kv * HEAD_DIM, HEAD_DIM), kv_width)

    local = [
        pltpu.make_async_copy(k_ref.at[0, :, kv_columns], kbuf.at[0, s], local_sem.at[0]),
        pltpu.make_async_copy(v_ref.at[0, :, kv_columns], vbuf.at[0, s], local_sem.at[1]),
        pltpu.make_async_copy(clip_ref, own_clip, local_sem.at[2]),
        pltpu.make_async_copy(q_ref.at[0], qbuf, local_sem.at[3]),
    ]
    for copy in local:
        copy.start()

    turn = 2 * (2 * me // n) - 1

    def chunk_at(step):
        return lax.rem(me + turn * (step + 1) + 2 * n, n)

    def w_copy(i):
        start = chunk_at(i // pieces) * chunk + lax.rem(i, pieces) * width
        return pltpu.make_async_copy(
            w_ref.at[:, pl.ds(pl.multiple_of(start, HEAD_DIM), width)], wbuf.at[i], w_sem.at[i]
        )

    barrier = pltpu.get_barrier_semaphore()
    for j in range(1, WINDOW):
        @pl.when(c >= j)
        def _():
            pl.semaphore_signal(barrier, inc=1, device_id={"span": c - j}, device_id_type=MESH)
    for d in range(1, seqs):
        pl.semaphore_signal(
            barrier, inc=1, device_id={"seq": lax.rem(s + d, seqs)}, device_id_type=MESH
        )

    @pl.when(me > 0)
    def _():
        pl.semaphore_signal(barrier, inc=1, device_id={"mp": me - 1}, device_id_type=MESH)

    @pl.when(me < n - 1)
    def _():
        pl.semaphore_signal(barrier, inc=1, device_id={"mp": me + 1}, device_id_type=MESH)

    def start_w(i, carry):
        w_copy(i).start()
        return carry

    lax.fori_loop(0, steps, start_w, 0)

    for j in range(1, WINDOW):
        @pl.when(c < j)
        def _():
            kbuf[j] = jnp.zeros(kbuf.shape[1:], kbuf.dtype)
            vbuf[j] = jnp.zeros(vbuf.shape[1:], vbuf.dtype)

    local[2].wait()
    clips[s] = jnp.broadcast_to(own_clip[...], clips.shape[1:])
    local[0].wait()
    local[1].wait()
    later_spans = jnp.minimum(spans - 1 - c, WINDOW - 1)
    z_neighbours = jnp.minimum(me, 1) + jnp.minimum(n - 1 - me, 1)
    pl.semaphore_wait(barrier, seqs - 1 + later_spans + z_neighbours)

    bufs = (kbuf, vbuf)

    def to_span(j, a):
        return pltpu.make_async_remote_copy(
            src_ref=bufs[a].at[0, s],
            dst_ref=bufs[a].at[j, s],
            send_sem=span_send.at[j, a],
            recv_sem=kv_recv.at[j, s, a],
            device_id={"span": c + j},
            device_id_type=MESH,
        )

    def to_seq(j, d, a):
        return pltpu.make_async_remote_copy(
            src_ref=bufs[a].at[j, s],
            dst_ref=bufs[a].at[j, s],
            send_sem=seq_send.at[j, d, a],
            recv_sem=kv_recv.at[j, s, a],
            device_id={"seq": lax.rem(s + d, seqs)},
            device_id_type=MESH,
        )

    def arrival(j, s2, a):
        return pltpu.make_async_remote_copy(
            src_ref=bufs[a].at[j, s2],
            dst_ref=bufs[a].at[j, s2],
            send_sem=seq_send.at[0, 0, a],
            recv_sem=kv_recv.at[j, s2, a],
            device_id={"seq": s2},
            device_id_type=MESH,
        )

    def clip_copy(d, source):
        return pltpu.make_async_remote_copy(
            src_ref=clips.at[source],
            dst_ref=clips.at[source],
            send_sem=clip_send.at[d],
            recv_sem=clip_recv.at[source],
            device_id={"seq": lax.rem(s + d, seqs)},
            device_id_type=MESH,
        )

    for a in range(2):
        for j in range(WINDOW - 1, 0, -1):
            @pl.when(c + j < spans)
            def _():
                to_span(j, a).start()
    for d in range(1, seqs):
        clip_copy(d, s).start()
    for a in range(2):
        for d in range(1, seqs):
            to_seq(0, d, a).start()

    def relay(a):
        for j in range(1, WINDOW):
            @pl.when(c >= j)
            def _():
                arrival(j, s, a).wait_recv()
                for d in range(1, seqs):
                    to_seq(j, d, a).start()

    def await_others(a):
        for d in range(1, seqs):
            arrival(0, lax.rem(s + d, seqs), a).wait_recv()
        for j in range(1, WINDOW):
            @pl.when(c >= j)
            def _():
                for d in range(1, seqs):
                    arrival(j, lax.rem(s + d, seqs), a).wait_recv()

    for d in range(1, seqs):
        clip_copy(d, lax.rem(s + d, seqs)).wait_recv()
    own = jnp.broadcast_to(own_clip[...], (rows, rows)).astype(jnp.float32)
    own_column = own.T
    same = [
        jnp.broadcast_to(clips[s2, 0:1, :], (rows, rows)).astype(jnp.float32) == own_column
        for s2 in range(seqs)
    ]
    blocks = []
    for j in range(WINDOW):
        entry = mask_ref[c, jnp.maximum(c - j, 0)]
        seen = jnp.where((c >= j) & (entry == 1), 0.0, MASKED).astype(jnp.float32)
        for s2 in range(seqs):
            blocks.append(jnp.where(same[s2], seen, MASKED))
    bias = jnp.concatenate(blocks, axis=1)

    local[3].wait()
    relay(0)
    relay(1)
    await_others(0)

    scale = HEAD_DIM ** (-0.5)
    key_count = WINDOW * seqs * rows
    stacked = GROUP if head_count % GROUP == 0 else 1
    probabilities = []
    for h in range(0, head_count, stacked):
        if head_count % GROUP == 0:
            g = h // GROUP
            keys = kbuf[:, :, :, g * HEAD_DIM:(g + 1) * HEAD_DIM]
        else:
            at = (me * head_count + h) // GROUP - first_kv
            keys = kbuf[:, :, :, 0:HEAD_DIM]
            for g in range(1, kv_count):
                keys = jnp.where(at == g, kbuf[:, :, :, g * HEAD_DIM:(g + 1) * HEAD_DIM], keys)
        keys = keys.reshape(key_count, HEAD_DIM)
        q = jnp.concatenate(
            [qbuf[:, i * HEAD_DIM:(i + 1) * HEAD_DIM] for i in range(h, h + stacked)], axis=0
        )
        scores = lax.dot_general(
            q, keys, (((1,), (1,)), ((), ())), preferred_element_type=jnp.float32
        ) * scale
        scores = scores.reshape(stacked, rows, key_count) + bias[None]
        top = jnp.max(scores, axis=2, keepdims=True)
        p = jnp.exp(scores - top)
        total = jnp.sum(p, axis=2, keepdims=True)
        probabilities.append((
            p.astype(jnp.bfloat16).reshape(stacked * rows, key_count),
            total.reshape(stacked * rows, 1),
        ))
    await_others(1)
    for h, (p, total) in zip(range(0, head_count, stacked), probabilities):
        if head_count % GROUP == 0:
            g = h // GROUP
            values = vbuf[:, :, :, g * HEAD_DIM:(g + 1) * HEAD_DIM]
        else:
            at = (me * head_count + h) // GROUP - first_kv
            values = vbuf[:, :, :, 0:HEAD_DIM]
            for g in range(1, kv_count):
                values = jnp.where(at == g, vbuf[:, :, :, g * HEAD_DIM:(g + 1) * HEAD_DIM], values)
        values = values.reshape(key_count, HEAD_DIM)
        o = jnp.dot(p, values, preferred_element_type=jnp.float32) / total
        o = o.astype(jnp.bfloat16)
        for i in range(stacked):
            att[:, (h + i) * HEAD_DIM:(h + i + 1) * HEAD_DIM] = o[i * rows:(i + 1) * rows]

    def pass_on(way, at):
        return pltpu.make_async_remote_copy(
            src_ref=sendbuf.at[at],
            dst_ref=recvbuf.at[way, at],
            send_sem=sum_send.at[at],
            recv_sem=sum_recv.at[way, at],
            device_id={"mp": me + 1 - 2 * way},
            device_id_type=MESH,
        )

    def project(i, carry):
        to = chunk_at(i // pieces)
        at = to * pieces + lax.rem(i, pieces)
        w_copy(i).wait()
        product = jnp.dot(att[...], wbuf[i], preferred_element_type=jnp.float32)
        part[at] = product

        @pl.when((me == 0) & (to > 0))
        def _():
            sendbuf[at] = product.astype(sendbuf.dtype)
            pass_on(0, at).start()

        @pl.when((me == n - 1) & (to < n - 1))
        def _():
            sendbuf[at] = product.astype(sendbuf.dtype)
            pass_on(1, at).start()

        return carry

    lax.fori_loop(0, steps, project, 0)

    lag = min(pieces, 3)

    def relay_sums(i, carry):
        k = jnp.maximum(i - lag * (me - 1), 0)
        up_chunk = n - 1 - k // pieces
        up = up_chunk * pieces + lax.rem(k, pieces)

        @pl.when((me > 0) & (i >= lag * (me - 1)) & (up_chunk > me))
        def _():
            pass_on(0, up).wait_recv()
            sendbuf[up] = (part[up] + recvbuf[0, up].astype(jnp.float32)).astype(sendbuf.dtype)
            pass_on(0, up).start()

        down = jnp.maximum(i - lag * (n - 2 - me), 0)

        @pl.when((me < n - 1) & (i >= lag * (n - 2 - me)) & (down // pieces < me))
        def _():
            pass_on(1, down).wait_recv()
            sendbuf[down] = (part[down] + recvbuf[1, down].astype(jnp.float32)).astype(sendbuf.dtype)
            pass_on(1, down).start()

        return carry

    lax.fori_loop(0, (n - 2) * pieces, relay_sums, 0)

    def out_copy(i):
        return pltpu.make_async_copy(
            outbuf.at[i], out_ref.at[0, :, pl.ds(i * width, width)], out_sem.at[i]
        )

    for i in range(pieces):
        at = me * pieces + i

        @pl.when(me > 0)
        def _():
            pass_on(0, at).wait_recv()
            part[at] += recvbuf[0, at].astype(jnp.float32)

        @pl.when(me < n - 1)
        def _():
            pass_on(1, at).wait_recv()
            part[at] += recvbuf[1, at].astype(jnp.float32)

        outbuf[i] = part[at].astype(outbuf.dtype)
        out_copy(i).start()

    for a in range(2):
        for j in range(1, WINDOW):
            @pl.when(c + j < spans)
            def _():
                to_span(j, a).wait_send()
            @pl.when(c >= j)
            def _():
                for d in range(1, seqs):
                    to_seq(j, d, a).wait_send()
        for d in range(1, seqs):
            to_seq(0, d, a).wait_send()
    for d in range(1, seqs):
        clip_copy(d, s).wait_send()

    def sent(i, carry):
        @pl.when(i // pieces != me)
        def _():
            pass_on(0, i).wait_send()

        return carry

    lax.fori_loop(0, steps, sent, 0)
    for i in range(pieces):
        out_copy(i).wait()


def on_device(queries, keys, values, clip_ids, block_mask, out_weight):
    spans = lax.axis_size("span")
    seqs = lax.axis_size("seq")
    n = lax.axis_size("mp")
    _, rows, local_width = queries.shape
    head_count = local_width // HEAD_DIM
    kv_total = keys.shape[2] // HEAD_DIM
    firsts = [m * head_count // GROUP for m in range(n)]
    lasts = [((m + 1) * head_count - 1) // GROUP for m in range(n)]
    kv_count = max(b - a + 1 for a, b in zip(firsts, lasts))
    kv_width = kv_count * HEAD_DIM
    depth, out_width = out_weight.shape
    chunk = out_width // n
    width = 256 if chunk % 256 == 0 else HEAD_DIM
    pieces = chunk // width
    bf16 = jnp.bfloat16
    hbm = pl.BlockSpec(memory_space=pl.ANY)
    return pl.pallas_call(
        functools.partial(kernel, spans, seqs, n, pieces, kv_count, kv_total),
        out_shape=jax.ShapeDtypeStruct((1, rows, chunk), bf16),
        in_specs=[hbm, hbm, hbm, hbm, pl.BlockSpec(memory_space=pltpu.SMEM), hbm],
        out_specs=hbm,
        scratch_shapes=[
            pltpu.VMEM((rows, local_width), bf16),
            pltpu.VMEM((WINDOW, seqs, rows, kv_width), bf16),
            pltpu.VMEM((WINDOW, seqs, rows, kv_width), bf16),
            pltpu.VMEM((1, rows), jnp.int32),
            pltpu.VMEM((seqs, 8, rows), jnp.int32),
            pltpu.VMEM((n * pieces, depth, width), bf16),
            pltpu.VMEM((rows, local_width), bf16),
            pltpu.VMEM((n * pieces, rows, width), jnp.float32),
            pltpu.VMEM((n * pieces, rows, width), bf16),
            pltpu.VMEM((2, n * pieces, rows, width), bf16),
            pltpu.VMEM((pieces, rows, width), bf16),
            pltpu.SemaphoreType.DMA((4,)),
            pltpu.SemaphoreType.DMA((n * pieces,)),
            pltpu.SemaphoreType.DMA((WINDOW, 2)),
            pltpu.SemaphoreType.DMA((WINDOW, seqs, 2)),
            pltpu.SemaphoreType.DMA((WINDOW, seqs, 2)),
            pltpu.SemaphoreType.DMA((seqs,)),
            pltpu.SemaphoreType.DMA((seqs,)),
            pltpu.SemaphoreType.DMA((n * pieces,)),
            pltpu.SemaphoreType.DMA((2, n * pieces)),
            pltpu.SemaphoreType.DMA((pieces,)),
        ],
        compiler_params=pltpu.CompilerParams(
            collective_id=0, has_side_effects=True, vmem_limit_bytes=64 * 1024 * 1024
        ),
    )(queries, keys, values, clip_ids.reshape(1, rows), block_mask, out_weight)


def solution(mesh):
    in_specs = (
        P("span", "seq", "mp"),
        P("span", "seq", None),
        P("span", "seq", None),
        P("seq"),
        P(),
        P("mp", None),
    )
    out_specs = P("span", "seq", "mp")
    return jax.shard_map(
        on_device, mesh=mesh, in_specs=in_specs, out_specs=out_specs, check_vma=False
    )
```

```python
import functools
import jax
import jax.numpy as jnp
from jax import lax
from jax.experimental import pallas as pl
from jax.experimental.pallas import tpu as pltpu
from jax.sharding import PartitionSpec as P

HEAD_DIM = 128
WINDOW = 3
GROUP = 6
MASKED = -1e30
MESH = pl.DeviceIdType.MESH


def kernel(
    spans, seqs, n, pieces, kv_count, kv_total,
    q_ref, k_ref, v_ref, clip_ref, mask_ref, w_ref, out_ref,
    qbuf, kbuf, vbuf, own_clip, mask, clips, wbuf, att, part, sendbuf, recvbuf, outbuf,
    local_sem, w_sem, span_send, seq_send, kv_recv, clip_send, clip_recv, sum_send, sum_recv, out_sem,
):
    rows, local_width = qbuf.shape
    head_count = local_width // HEAD_DIM
    width = wbuf.shape[2]
    chunk = width * pieces
    kv_width = kv_count * HEAD_DIM
    steps = n * pieces
    c = lax.axis_index("span")
    s = lax.axis_index("seq")
    me = lax.axis_index("mp")

    first_kv = jnp.minimum(me * head_count // GROUP, kv_total - kv_count)
    kv_columns = pl.ds(pl.multiple_of(first_kv * HEAD_DIM, HEAD_DIM), kv_width)

    local = [
        pltpu.make_async_copy(k_ref.at[0, :, kv_columns], kbuf.at[0, s], local_sem.at[0]),
        pltpu.make_async_copy(v_ref.at[0, :, kv_columns], vbuf.at[0, s], local_sem.at[1]),
        pltpu.make_async_copy(clip_ref, own_clip, local_sem.at[2]),
        pltpu.make_async_copy(q_ref.at[0], qbuf, local_sem.at[3]),
        pltpu.make_async_copy(mask_ref, mask, local_sem.at[4]),
    ]
    for copy in local:
        copy.start()

    up_count = (n - 1 - me) * pieces
    down_count = me * pieces
    both = jnp.minimum(up_count, down_count)

    def piece_at(i):
        k = jnp.where(i < 2 * both, i // 2, i - both)
        goes_up = jnp.where(i < 2 * both, 1 - lax.rem(i, 2), jnp.where(up_count > down_count, 1, 0))
        moving = jnp.where(goes_up == 1, n - 1 - k // pieces, k // pieces)
        to = jnp.where(i < up_count + down_count, moving, me)
        return to, lax.rem(k, pieces)

    def w_copy(i):
        to, piece = piece_at(i)
        start = to * chunk + piece * width
        return pltpu.make_async_copy(
            w_ref.at[:, pl.ds(pl.multiple_of(start, HEAD_DIM), width)], wbuf.at[i], w_sem.at[i]
        )

    barrier = pltpu.get_barrier_semaphore()
    for j in range(1, WINDOW):
        @pl.when(c >= j)
        def _():
            pl.semaphore_signal(barrier, inc=1, device_id={"span": c - j}, device_id_type=MESH)
    for d in range(1, seqs):
        pl.semaphore_signal(
            barrier, inc=1, device_id={"seq": lax.rem(s + d, seqs)}, device_id_type=MESH
        )

    @pl.when(me > 0)
    def _():
        pl.semaphore_signal(barrier, inc=1, device_id={"mp": me - 1}, device_id_type=MESH)

    @pl.when(me < n - 1)
    def _():
        pl.semaphore_signal(barrier, inc=1, device_id={"mp": me + 1}, device_id_type=MESH)

    def start_w(i, carry):
        w_copy(i).start()
        return carry

    lax.fori_loop(0, steps, start_w, 0)

    for j in range(1, WINDOW):
        @pl.when(c < j)
        def _():
            kbuf[j] = jnp.zeros(kbuf.shape[1:], kbuf.dtype)
            vbuf[j] = jnp.zeros(vbuf.shape[1:], vbuf.dtype)

    local[2].wait()
    clips[s] = jnp.broadcast_to(own_clip[...], clips.shape[1:])
    local[0].wait()
    local[1].wait()
    later_spans = jnp.minimum(spans - 1 - c, WINDOW - 1)
    z_neighbours = jnp.minimum(me, 1) + jnp.minimum(n - 1 - me, 1)
    pl.semaphore_wait(barrier, seqs - 1 + later_spans + z_neighbours)

    bufs = (kbuf, vbuf)

    def to_span(j, a):
        return pltpu.make_async_remote_copy(
            src_ref=bufs[a].at[0, s],
            dst_ref=bufs[a].at[j, s],
            send_sem=span_send.at[j, a],
            recv_sem=kv_recv.at[j, s, a],
            device_id={"span": c + j},
            device_id_type=MESH,
        )

    def to_seq(j, d, a):
        return pltpu.make_async_remote_copy(
            src_ref=bufs[a].at[j, s],
            dst_ref=bufs[a].at[j, s],
            send_sem=seq_send.at[j, d, a],
            recv_sem=kv_recv.at[j, s, a],
            device_id={"seq": lax.rem(s + d, seqs)},
            device_id_type=MESH,
        )

    def arrival(j, s2, a):
        return pltpu.make_async_remote_copy(
            src_ref=bufs[a].at[j, s2],
            dst_ref=bufs[a].at[j, s2],
            send_sem=seq_send.at[0, 0, a],
            recv_sem=kv_recv.at[j, s2, a],
            device_id={"seq": s2},
            device_id_type=MESH,
        )

    def clip_copy(d, source):
        return pltpu.make_async_remote_copy(
            src_ref=clips.at[source],
            dst_ref=clips.at[source],
            send_sem=clip_send.at[d],
            recv_sem=clip_recv.at[source],
            device_id={"seq": lax.rem(s + d, seqs)},
            device_id_type=MESH,
        )

    for a in range(2):
        for j in range(WINDOW - 1, 0, -1):
            @pl.when(c + j < spans)
            def _():
                to_span(j, a).start()
    for d in range(1, seqs):
        clip_copy(d, s).start()
    for a in range(2):
        for d in range(1, seqs):
            to_seq(0, d, a).start()

    def relay(a):
        for j in range(1, WINDOW):
            @pl.when(c >= j)
            def _():
                arrival(j, s, a).wait_recv()
                for d in range(1, seqs):
                    to_seq(j, d, a).start()

    def await_others(a):
        for d in range(1, seqs):
            arrival(0, lax.rem(s + d, seqs), a).wait_recv()
        for j in range(1, WINDOW):
            @pl.when(c >= j)
            def _():
                for d in range(1, seqs):
                    arrival(j, lax.rem(s + d, seqs), a).wait_recv()

    for d in range(1, seqs):
        clip_copy(d, lax.rem(s + d, seqs)).wait_recv()
    own = jnp.broadcast_to(own_clip[...], (rows, rows)).astype(jnp.float32)
    own_column = own.T
    same = [
        jnp.broadcast_to(clips[s2, 0:1, :], (rows, rows)).astype(jnp.float32) == own_column
        for s2 in range(seqs)
    ]
    local[4].wait()
    blocks = []
    for j in range(WINDOW):
        entry = mask[c, jnp.maximum(c - j, 0)]
        seen = jnp.where((c >= j) & (entry == 1), 0.0, MASKED).astype(jnp.float32)
        for s2 in range(seqs):
            blocks.append(jnp.where(same[s2], seen, MASKED))
    bias = jnp.concatenate(blocks, axis=1)

    local[3].wait()
    relay(0)
    relay(1)
    await_others(0)

    scale = HEAD_DIM ** (-0.5)
    key_count = WINDOW * seqs * rows
    stacked = GROUP if head_count % GROUP == 0 else 1
    probabilities = []
    for h in range(0, head_count, stacked):
        if head_count % GROUP == 0:
            g = h // GROUP
            keys = kbuf[:, :, :, g * HEAD_DIM:(g + 1) * HEAD_DIM]
        else:
            at = (me * head_count + h) // GROUP - first_kv
            keys = kbuf[:, :, :, 0:HEAD_DIM]
            for g in range(1, kv_count):
                keys = jnp.where(at == g, kbuf[:, :, :, g * HEAD_DIM:(g + 1) * HEAD_DIM], keys)
        keys = keys.reshape(key_count, HEAD_DIM)
        q = jnp.concatenate(
            [qbuf[:, i * HEAD_DIM:(i + 1) * HEAD_DIM] for i in range(h, h + stacked)], axis=0
        )
        scores = lax.dot_general(
            q, keys, (((1,), (1,)), ((), ())), preferred_element_type=jnp.float32
        ) * scale
        scores = scores.reshape(stacked, rows, key_count) + bias[None]
        top = jnp.max(scores, axis=2, keepdims=True)
        p = jnp.exp(scores - top)
        total = jnp.sum(p, axis=2, keepdims=True)
        probabilities.append((
            p.astype(jnp.bfloat16).reshape(stacked * rows, key_count),
            total.reshape(stacked * rows, 1),
        ))
    await_others(1)
    for h, (p, total) in zip(range(0, head_count, stacked), probabilities):
        if head_count % GROUP == 0:
            g = h // GROUP
            values = vbuf[:, :, :, g * HEAD_DIM:(g + 1) * HEAD_DIM]
        else:
            at = (me * head_count + h) // GROUP - first_kv
            values = vbuf[:, :, :, 0:HEAD_DIM]
            for g in range(1, kv_count):
                values = jnp.where(at == g, vbuf[:, :, :, g * HEAD_DIM:(g + 1) * HEAD_DIM], values)
        values = values.reshape(key_count, HEAD_DIM)
        o = jnp.dot(p, values, preferred_element_type=jnp.float32) / total
        o = o.astype(jnp.bfloat16)
        for i in range(stacked):
            att[:, (h + i) * HEAD_DIM:(h + i + 1) * HEAD_DIM] = o[i * rows:(i + 1) * rows]

    def pass_on(way, at):
        return pltpu.make_async_remote_copy(
            src_ref=sendbuf.at[at],
            dst_ref=recvbuf.at[way, at],
            send_sem=sum_send.at[at],
            recv_sem=sum_recv.at[way, at],
            device_id={"mp": me + 1 - 2 * way},
            device_id_type=MESH,
        )

    def project(i):
        to, piece = piece_at(i)
        at = to * pieces + piece
        w_copy(i).wait()
        product = jnp.dot(att[...], wbuf[i], preferred_element_type=jnp.float32)
        part[at] = product

        @pl.when((me == 0) & (to > 0))
        def _():
            sendbuf[at] = product.astype(sendbuf.dtype)
            pass_on(0, at).start()

        @pl.when((me == n - 1) & (to < n - 1))
        def _():
            sendbuf[at] = product.astype(sendbuf.dtype)
            pass_on(1, at).start()

    up_lag = 2 * me - 1
    down_lag = 2 * (n - 1 - me) - 1

    def relay_sums(m):
        up = (n - 1) * pieces - jnp.maximum(m - up_lag, 0) // pieces * pieces + lax.rem(
            jnp.maximum(m - up_lag, 0), pieces
        )

        @pl.when((me > 0) & (m >= up_lag) & (m - up_lag < up_count))
        def _():
            pass_on(0, up).wait_recv()
            sendbuf[up] = (part[up] + recvbuf[0, up].astype(jnp.float32)).astype(sendbuf.dtype)
            pass_on(0, up).start()

        down = jnp.maximum(m - down_lag, 0)

        @pl.when((me < n - 1) & (m >= down_lag) & (m - down_lag < down_count))
        def _():
            pass_on(1, down).wait_recv()
            sendbuf[down] = (part[down] + recvbuf[1, down].astype(jnp.float32)).astype(sendbuf.dtype)
            pass_on(1, down).start()

    def project_and_relay(m, carry):
        project(2 * m)
        project(2 * m + 1)
        relay_sums(m)
        return carry

    def relay_only(m, carry):
        relay_sums(m)
        return carry

    lax.fori_loop(0, steps // 2, project_and_relay, 0)
    last = max((n - 1 - z) * pieces + 2 * z - 1 for z in range(1, n))
    lax.fori_loop(steps // 2, last, relay_only, 0)

    def out_copy(i):
        return pltpu.make_async_copy(
            outbuf.at[i], out_ref.at[0, :, pl.ds(i * width, width)], out_sem.at[i]
        )

    for i in range(pieces):
        at = me * pieces + i

        @pl.when(me > 0)
        def _():
            pass_on(0, at).wait_recv()
            part[at] += recvbuf[0, at].astype(jnp.float32)

        @pl.when(me < n - 1)
        def _():
            pass_on(1, at).wait_recv()
            part[at] += recvbuf[1, at].astype(jnp.float32)

        outbuf[i] = part[at].astype(outbuf.dtype)
        out_copy(i).start()

    for a in range(2):
        for j in range(1, WINDOW):
            @pl.when(c + j < spans)
            def _():
                to_span(j, a).wait_send()
            @pl.when(c >= j)
            def _():
                for d in range(1, seqs):
                    to_seq(j, d, a).wait_send()
        for d in range(1, seqs):
            to_seq(0, d, a).wait_send()
    for d in range(1, seqs):
        clip_copy(d, s).wait_send()

    def sent(i, carry):
        @pl.when(i // pieces != me)
        def _():
            pass_on(0, i).wait_send()

        return carry

    lax.fori_loop(0, steps, sent, 0)
    for i in range(pieces):
        out_copy(i).wait()


def on_device(queries, keys, values, clip_ids, block_mask, out_weight):
    spans = lax.axis_size("span")
    seqs = lax.axis_size("seq")
    n = lax.axis_size("mp")
    _, rows, local_width = queries.shape
    head_count = local_width // HEAD_DIM
    kv_total = keys.shape[2] // HEAD_DIM
    firsts = [m * head_count // GROUP for m in range(n)]
    lasts = [((m + 1) * head_count - 1) // GROUP for m in range(n)]
    kv_count = max(b - a + 1 for a, b in zip(firsts, lasts))
    kv_width = kv_count * HEAD_DIM
    depth, out_width = out_weight.shape
    chunk = out_width // n
    width = 256 if chunk % 256 == 0 else HEAD_DIM
    pieces = chunk // width
    bf16 = jnp.bfloat16
    hbm = pl.BlockSpec(memory_space=pl.ANY)
    return pl.pallas_call(
        functools.partial(kernel, spans, seqs, n, pieces, kv_count, kv_total),
        out_shape=jax.ShapeDtypeStruct((1, rows, chunk), bf16),
        in_specs=[hbm] * 6,
        out_specs=hbm,
        scratch_shapes=[
            pltpu.VMEM((rows, local_width), bf16),
            pltpu.VMEM((WINDOW, seqs, rows, kv_width), bf16),
            pltpu.VMEM((WINDOW, seqs, rows, kv_width), bf16),
            pltpu.VMEM((1, rows), jnp.int32),
            pltpu.SMEM(block_mask.shape, jnp.int32),
            pltpu.VMEM((seqs, 8, rows), jnp.int32),
            pltpu.VMEM((n * pieces, depth, width), bf16),
            pltpu.VMEM((rows, local_width), bf16),
            pltpu.VMEM((n * pieces, rows, width), jnp.float32),
            pltpu.VMEM((n * pieces, rows, width), bf16),
            pltpu.VMEM((2, n * pieces, rows, width), bf16),
            pltpu.VMEM((pieces, rows, width), bf16),
            pltpu.SemaphoreType.DMA((5,)),
            pltpu.SemaphoreType.DMA((n * pieces,)),
            pltpu.SemaphoreType.DMA((WINDOW, 2)),
            pltpu.SemaphoreType.DMA((WINDOW, seqs, 2)),
            pltpu.SemaphoreType.DMA((WINDOW, seqs, 2)),
            pltpu.SemaphoreType.DMA((seqs,)),
            pltpu.SemaphoreType.DMA((seqs,)),
            pltpu.SemaphoreType.DMA((n * pieces,)),
            pltpu.SemaphoreType.DMA((2, n * pieces)),
            pltpu.SemaphoreType.DMA((pieces,)),
        ],
        compiler_params=pltpu.CompilerParams(
            collective_id=0, has_side_effects=True, vmem_limit_bytes=64 * 1024 * 1024
        ),
    )(queries, keys, values, clip_ids.reshape(1, rows), block_mask, out_weight)


def solution(mesh):
    in_specs = (
        P("span", "seq", "mp"),
        P("span", "seq", None),
        P("span", "seq", None),
        P("seq"),
        P(),
        P("mp", None),
    )
    out_specs = P("span", "seq", "mp")
    return jax.shard_map(
        on_device, mesh=mesh, in_specs=in_specs, out_specs=out_specs, check_vma=False
    )
```

```python
import functools
import jax
import jax.numpy as jnp
from jax import lax
from jax.experimental import pallas as pl
from jax.experimental.pallas import tpu as pltpu
from jax.sharding import PartitionSpec as P

HEAD_DIM = 128
WINDOW = 3
GROUP = 6
MASKED = -1e30
MESH = pl.DeviceIdType.MESH


def kernel(
    spans, seqs, n, pieces, kv_count, kv_total,
    q_ref, k_ref, v_ref, clip_ref, mask_ref, w_ref, out_ref,
    qbuf, kbuf, vbuf, own_clip, mask, clips, wbuf, att, part, sendbuf, recvbuf, outbuf,
    local_sem, w_sem, span_send, seq_send, kv_recv, clip_send, clip_recv, sum_send, sum_recv, out_sem,
):
    rows, local_width = qbuf.shape
    head_count = local_width // HEAD_DIM
    width = wbuf.shape[2]
    chunk = width * pieces
    kv_width = kv_count * HEAD_DIM
    steps = n * pieces
    c = lax.axis_index("span")
    s = lax.axis_index("seq")
    me = lax.axis_index("mp")

    first_kv = jnp.minimum(me * head_count // GROUP, kv_total - kv_count)
    kv_columns = pl.ds(pl.multiple_of(first_kv * HEAD_DIM, HEAD_DIM), kv_width)

    local = [
        pltpu.make_async_copy(k_ref.at[0, :, kv_columns], kbuf.at[0, s], local_sem.at[0]),
        pltpu.make_async_copy(v_ref.at[0, :, kv_columns], vbuf.at[0, s], local_sem.at[1]),
        pltpu.make_async_copy(clip_ref, own_clip, local_sem.at[2]),
        pltpu.make_async_copy(q_ref.at[0], qbuf, local_sem.at[3]),
        pltpu.make_async_copy(mask_ref, mask, local_sem.at[4]),
    ]
    for copy in local:
        copy.start()

    up_count = (n - 1 - me) * pieces
    down_count = me * pieces
    both = jnp.minimum(up_count, down_count)

    def piece_at(i):
        k = jnp.where(i < 2 * both, i // 2, i - both)
        goes_up = jnp.where(i < 2 * both, 1 - lax.rem(i, 2), jnp.where(up_count > down_count, 1, 0))
        moving = jnp.where(goes_up == 1, n - 1 - k // pieces, k // pieces)
        to = jnp.where(i < up_count + down_count, moving, me)
        return to, lax.rem(k, pieces)

    def w_copy(i):
        to, piece = piece_at(i)
        start = to * chunk + piece * width
        return pltpu.make_async_copy(
            w_ref.at[:, pl.ds(pl.multiple_of(start, HEAD_DIM), width)], wbuf.at[i], w_sem.at[i]
        )

    barrier = pltpu.get_barrier_semaphore()
    for j in range(1, WINDOW):
        @pl.when(c >= j)
        def _():
            pl.semaphore_signal(barrier, inc=1, device_id={"span": c - j}, device_id_type=MESH)
    for d in range(1, seqs):
        pl.semaphore_signal(
            barrier, inc=1, device_id={"seq": lax.rem(s + d, seqs)}, device_id_type=MESH
        )

    @pl.when(me > 0)
    def _():
        pl.semaphore_signal(barrier, inc=1, device_id={"mp": me - 1}, device_id_type=MESH)

    @pl.when(me < n - 1)
    def _():
        pl.semaphore_signal(barrier, inc=1, device_id={"mp": me + 1}, device_id_type=MESH)

    def start_w(i, carry):
        w_copy(i).start()
        return carry

    early = min(steps, 8)
    lax.fori_loop(0, early, start_w, 0)

    for j in range(1, WINDOW):
        @pl.when(c < j)
        def _():
            kbuf[j] = jnp.zeros(kbuf.shape[1:], kbuf.dtype)
            vbuf[j] = jnp.zeros(vbuf.shape[1:], vbuf.dtype)

    local[2].wait()
    clips[s] = jnp.broadcast_to(own_clip[...], clips.shape[1:])
    local[0].wait()
    local[1].wait()
    later_spans = jnp.minimum(spans - 1 - c, WINDOW - 1)
    z_neighbours = jnp.minimum(me, 1) + jnp.minimum(n - 1 - me, 1)
    pl.semaphore_wait(barrier, seqs - 1 + later_spans + z_neighbours)

    bufs = (kbuf, vbuf)

    def to_span(j, a):
        return pltpu.make_async_remote_copy(
            src_ref=bufs[a].at[0, s],
            dst_ref=bufs[a].at[j, s],
            send_sem=span_send.at[j, a],
            recv_sem=kv_recv.at[j, s, a],
            device_id={"span": c + j},
            device_id_type=MESH,
        )

    def to_seq(j, d, a):
        return pltpu.make_async_remote_copy(
            src_ref=bufs[a].at[j, s],
            dst_ref=bufs[a].at[j, s],
            send_sem=seq_send.at[j, d, a],
            recv_sem=kv_recv.at[j, s, a],
            device_id={"seq": lax.rem(s + d, seqs)},
            device_id_type=MESH,
        )

    def arrival(j, s2, a):
        return pltpu.make_async_remote_copy(
            src_ref=bufs[a].at[j, s2],
            dst_ref=bufs[a].at[j, s2],
            send_sem=seq_send.at[0, 0, a],
            recv_sem=kv_recv.at[j, s2, a],
            device_id={"seq": s2},
            device_id_type=MESH,
        )

    def clip_copy(d, source):
        return pltpu.make_async_remote_copy(
            src_ref=clips.at[source],
            dst_ref=clips.at[source],
            send_sem=clip_send.at[d],
            recv_sem=clip_recv.at[source],
            device_id={"seq": lax.rem(s + d, seqs)},
            device_id_type=MESH,
        )

    for a in range(2):
        for j in range(WINDOW - 1, 0, -1):
            @pl.when(c + j < spans)
            def _():
                to_span(j, a).start()
    for d in range(1, seqs):
        clip_copy(d, s).start()
    for a in range(2):
        for d in range(1, seqs):
            to_seq(0, d, a).start()

    def relay(a):
        for j in range(1, WINDOW):
            @pl.when(c >= j)
            def _():
                arrival(j, s, a).wait_recv()
                for d in range(1, seqs):
                    to_seq(j, d, a).start()

    def await_others(a):
        for d in range(1, seqs):
            arrival(0, lax.rem(s + d, seqs), a).wait_recv()
        for j in range(1, WINDOW):
            @pl.when(c >= j)
            def _():
                for d in range(1, seqs):
                    arrival(j, lax.rem(s + d, seqs), a).wait_recv()

    for d in range(1, seqs):
        clip_copy(d, lax.rem(s + d, seqs)).wait_recv()
    own = jnp.broadcast_to(own_clip[...], (rows, rows)).astype(jnp.float32)
    own_column = own.T
    same = [
        jnp.broadcast_to(clips[s2, 0:1, :], (rows, rows)).astype(jnp.float32) == own_column
        for s2 in range(seqs)
    ]
    local[4].wait()
    blocks = []
    for j in range(WINDOW):
        entry = mask[c, jnp.maximum(c - j, 0)]
        seen = jnp.where((c >= j) & (entry == 1), 0.0, MASKED).astype(jnp.float32)
        for s2 in range(seqs):
            blocks.append(jnp.where(same[s2], seen, MASKED))
    bias = jnp.concatenate(blocks, axis=1)

    local[3].wait()
    relay(0)
    relay(1)
    await_others(0)

    scale = HEAD_DIM ** (-0.5)
    key_count = WINDOW * seqs * rows
    stacked = GROUP if head_count % GROUP == 0 else 1
    probabilities = []
    for h in range(0, head_count, stacked):
        if head_count % GROUP == 0:
            g = h // GROUP
            keys = kbuf[:, :, :, g * HEAD_DIM:(g + 1) * HEAD_DIM]
        else:
            at = (me * head_count + h) // GROUP - first_kv
            keys = kbuf[:, :, :, 0:HEAD_DIM]
            for g in range(1, kv_count):
                keys = jnp.where(at == g, kbuf[:, :, :, g * HEAD_DIM:(g + 1) * HEAD_DIM], keys)
        keys = keys.reshape(key_count, HEAD_DIM)
        q = jnp.concatenate(
            [qbuf[:, i * HEAD_DIM:(i + 1) * HEAD_DIM] for i in range(h, h + stacked)], axis=0
        )
        scores = lax.dot_general(
            q, keys, (((1,), (1,)), ((), ())), preferred_element_type=jnp.float32
        ) * scale
        scores = scores.reshape(stacked, rows, key_count) + bias[None]
        top = jnp.max(scores, axis=2, keepdims=True)
        p = jnp.exp(scores - top)
        total = jnp.sum(p, axis=2, keepdims=True)
        probabilities.append((
            p.astype(jnp.bfloat16).reshape(stacked * rows, key_count),
            total.reshape(stacked * rows, 1),
        ))
    await_others(1)
    lax.fori_loop(early, steps, start_w, 0)
    for h, (p, total) in zip(range(0, head_count, stacked), probabilities):
        if head_count % GROUP == 0:
            g = h // GROUP
            values = vbuf[:, :, :, g * HEAD_DIM:(g + 1) * HEAD_DIM]
        else:
            at = (me * head_count + h) // GROUP - first_kv
            values = vbuf[:, :, :, 0:HEAD_DIM]
            for g in range(1, kv_count):
                values = jnp.where(at == g, vbuf[:, :, :, g * HEAD_DIM:(g + 1) * HEAD_DIM], values)
        values = values.reshape(key_count, HEAD_DIM)
        o = jnp.dot(p, values, preferred_element_type=jnp.float32) / total
        o = o.astype(jnp.bfloat16)
        for i in range(stacked):
            att[:, (h + i) * HEAD_DIM:(h + i + 1) * HEAD_DIM] = o[i * rows:(i + 1) * rows]

    def pass_on(way, at):
        return pltpu.make_async_remote_copy(
            src_ref=sendbuf.at[at],
            dst_ref=recvbuf.at[way, at],
            send_sem=sum_send.at[at],
            recv_sem=sum_recv.at[way, at],
            device_id={"mp": me + 1 - 2 * way},
            device_id_type=MESH,
        )

    def project(i):
        to, piece = piece_at(i)
        at = to * pieces + piece
        w_copy(i).wait()
        product = jnp.dot(att[...], wbuf[i], preferred_element_type=jnp.float32)
        part[at] = product

        @pl.when((me == 0) & (to > 0))
        def _():
            sendbuf[at] = product.astype(sendbuf.dtype)
            pass_on(0, at).start()

        @pl.when((me == n - 1) & (to < n - 1))
        def _():
            sendbuf[at] = product.astype(sendbuf.dtype)
            pass_on(1, at).start()

    up_lag = 2 * me - 1
    down_lag = 2 * (n - 1 - me) - 1

    def relay_sums(m):
        up = (n - 1) * pieces - jnp.maximum(m - up_lag, 0) // pieces * pieces + lax.rem(
            jnp.maximum(m - up_lag, 0), pieces
        )

        @pl.when((me > 0) & (m >= up_lag) & (m - up_lag < up_count))
        def _():
            pass_on(0, up).wait_recv()
            sendbuf[up] = (part[up] + recvbuf[0, up].astype(jnp.float32)).astype(sendbuf.dtype)
            pass_on(0, up).start()

        down = jnp.maximum(m - down_lag, 0)

        @pl.when((me < n - 1) & (m >= down_lag) & (m - down_lag < down_count))
        def _():
            pass_on(1, down).wait_recv()
            sendbuf[down] = (part[down] + recvbuf[1, down].astype(jnp.float32)).astype(sendbuf.dtype)
            pass_on(1, down).start()

    def project_and_relay(m, carry):
        project(2 * m)
        project(2 * m + 1)
        relay_sums(m)
        return carry

    def relay_only(m, carry):
        relay_sums(m)
        return carry

    lax.fori_loop(0, steps // 2, project_and_relay, 0)
    last = max((n - 1 - z) * pieces + 2 * z - 1 for z in range(1, n))
    lax.fori_loop(steps // 2, last, relay_only, 0)

    def out_copy(i):
        return pltpu.make_async_copy(
            outbuf.at[i], out_ref.at[0, :, pl.ds(i * width, width)], out_sem.at[i]
        )

    for i in range(pieces):
        at = me * pieces + i

        @pl.when(me > 0)
        def _():
            pass_on(0, at).wait_recv()
            part[at] += recvbuf[0, at].astype(jnp.float32)

        @pl.when(me < n - 1)
        def _():
            pass_on(1, at).wait_recv()
            part[at] += recvbuf[1, at].astype(jnp.float32)

        outbuf[i] = part[at].astype(outbuf.dtype)
        out_copy(i).start()

    for a in range(2):
        for j in range(1, WINDOW):
            @pl.when(c + j < spans)
            def _():
                to_span(j, a).wait_send()
            @pl.when(c >= j)
            def _():
                for d in range(1, seqs):
                    to_seq(j, d, a).wait_send()
        for d in range(1, seqs):
            to_seq(0, d, a).wait_send()
    for d in range(1, seqs):
        clip_copy(d, s).wait_send()

    def sent(i, carry):
        @pl.when(i // pieces != me)
        def _():
            pass_on(0, i).wait_send()

        return carry

    lax.fori_loop(0, steps, sent, 0)
    for i in range(pieces):
        out_copy(i).wait()


def on_device(queries, keys, values, clip_ids, block_mask, out_weight):
    spans = lax.axis_size("span")
    seqs = lax.axis_size("seq")
    n = lax.axis_size("mp")
    _, rows, local_width = queries.shape
    head_count = local_width // HEAD_DIM
    kv_total = keys.shape[2] // HEAD_DIM
    firsts = [m * head_count // GROUP for m in range(n)]
    lasts = [((m + 1) * head_count - 1) // GROUP for m in range(n)]
    kv_count = max(b - a + 1 for a, b in zip(firsts, lasts))
    kv_width = kv_count * HEAD_DIM
    depth, out_width = out_weight.shape
    chunk = out_width // n
    width = 256 if chunk % 256 == 0 else HEAD_DIM
    pieces = chunk // width
    bf16 = jnp.bfloat16
    hbm = pl.BlockSpec(memory_space=pl.ANY)
    return pl.pallas_call(
        functools.partial(kernel, spans, seqs, n, pieces, kv_count, kv_total),
        out_shape=jax.ShapeDtypeStruct((1, rows, chunk), bf16),
        in_specs=[hbm] * 6,
        out_specs=hbm,
        scratch_shapes=[
            pltpu.VMEM((rows, local_width), bf16),
            pltpu.VMEM((WINDOW, seqs, rows, kv_width), bf16),
            pltpu.VMEM((WINDOW, seqs, rows, kv_width), bf16),
            pltpu.VMEM((1, rows), jnp.int32),
            pltpu.SMEM(block_mask.shape, jnp.int32),
            pltpu.VMEM((seqs, 8, rows), jnp.int32),
            pltpu.VMEM((n * pieces, depth, width), bf16),
            pltpu.VMEM((rows, local_width), bf16),
            pltpu.VMEM((n * pieces, rows, width), jnp.float32),
            pltpu.VMEM((n * pieces, rows, width), bf16),
            pltpu.VMEM((2, n * pieces, rows, width), bf16),
            pltpu.VMEM((pieces, rows, width), bf16),
            pltpu.SemaphoreType.DMA((5,)),
            pltpu.SemaphoreType.DMA((n * pieces,)),
            pltpu.SemaphoreType.DMA((WINDOW, 2)),
            pltpu.SemaphoreType.DMA((WINDOW, seqs, 2)),
            pltpu.SemaphoreType.DMA((WINDOW, seqs, 2)),
            pltpu.SemaphoreType.DMA((seqs,)),
            pltpu.SemaphoreType.DMA((seqs,)),
            pltpu.SemaphoreType.DMA((n * pieces,)),
            pltpu.SemaphoreType.DMA((2, n * pieces)),
            pltpu.SemaphoreType.DMA((pieces,)),
        ],
        compiler_params=pltpu.CompilerParams(
            collective_id=0, has_side_effects=True, vmem_limit_bytes=64 * 1024 * 1024
        ),
    )(queries, keys, values, clip_ids.reshape(1, rows), block_mask, out_weight)


def solution(mesh):
    in_specs = (
        P("span", "seq", "mp"),
        P("span", "seq", None),
        P("span", "seq", None),
        P("seq"),
        P(),
        P("mp", None),
    )
    out_specs = P("span", "seq", "mp")
    return jax.shard_map(
        on_device, mesh=mesh, in_specs=in_specs, out_specs=out_specs, check_vma=False
    )
```

```python
import functools
import jax
import jax.numpy as jnp
from jax import lax
from jax.experimental import pallas as pl
from jax.experimental.pallas import tpu as pltpu
from jax.sharding import PartitionSpec as P

HEAD_DIM = 128
WINDOW = 3
GROUP = 6
MASKED = -1e30
MESH = pl.DeviceIdType.MESH


def kernel(
    spans, seqs, n, pieces, kv_count, kv_total,
    q_ref, k_ref, v_ref, clip_ref, mask_ref, w_ref, out_ref,
    qbuf, kbuf, vbuf, own_clip, mask, clips, wbuf, att, part, sendbuf, recvbuf, outbuf,
    local_sem, w_sem, span_send, seq_send, kv_recv, clip_send, clip_recv, sum_send, sum_recv, out_sem,
    att_send, att_recv, out_send, out_recv,
):
    rows, local_width = qbuf.shape
    head_count = local_width // HEAD_DIM
    width = wbuf.shape[2]
    half = width * pieces
    kv_width = kv_count * HEAD_DIM
    steps = n * pieces
    c = lax.axis_index("span")
    s = lax.axis_index("seq")
    me = lax.axis_index("mp")
    core = lax.rem(s, 2)
    sibling = {"seq": s + 1 - 2 * core}

    first_kv = jnp.minimum(me * head_count // GROUP, kv_total - kv_count)
    kv_columns = pl.ds(pl.multiple_of(first_kv * HEAD_DIM, HEAD_DIM), kv_width)

    local = [
        pltpu.make_async_copy(k_ref.at[0, :, kv_columns], kbuf.at[0, s], local_sem.at[0]),
        pltpu.make_async_copy(v_ref.at[0, :, kv_columns], vbuf.at[0, s], local_sem.at[1]),
        pltpu.make_async_copy(clip_ref, own_clip, local_sem.at[2]),
        pltpu.make_async_copy(q_ref.at[0], qbuf, local_sem.at[3]),
        pltpu.make_async_copy(mask_ref, mask, local_sem.at[4]),
    ]
    for copy in local:
        copy.start()

    up_count = (n - 1 - me) * pieces
    down_count = me * pieces
    both = jnp.minimum(up_count, down_count)

    def piece_at(i):
        k = jnp.where(i < 2 * both, i // 2, i - both)
        goes_up = jnp.where(i < 2 * both, 1 - lax.rem(i, 2), jnp.where(up_count > down_count, 1, 0))
        moving = jnp.where(goes_up == 1, n - 1 - k // pieces, k // pieces)
        to = jnp.where(i < up_count + down_count, moving, me)
        return to, lax.rem(k, pieces)

    def w_copy(i):
        to, piece = piece_at(i)
        start = (to * 2 + core) * half + piece * width
        return pltpu.make_async_copy(
            w_ref.at[:, pl.ds(pl.multiple_of(start, HEAD_DIM), width)], wbuf.at[i], w_sem.at[i]
        )

    barrier = pltpu.get_barrier_semaphore()
    for j in range(1, WINDOW):
        @pl.when(c >= j)
        def _():
            pl.semaphore_signal(barrier, inc=1, device_id={"span": c - j}, device_id_type=MESH)
    for d in range(1, seqs):
        pl.semaphore_signal(
            barrier, inc=1, device_id={"seq": lax.rem(s + d, seqs)}, device_id_type=MESH
        )

    @pl.when(me > 0)
    def _():
        pl.semaphore_signal(barrier, inc=1, device_id={"mp": me - 1}, device_id_type=MESH)

    @pl.when(me < n - 1)
    def _():
        pl.semaphore_signal(barrier, inc=1, device_id={"mp": me + 1}, device_id_type=MESH)

    def start_w(i, carry):
        w_copy(i).start()
        return carry

    lax.fori_loop(0, steps, start_w, 0)

    for j in range(1, WINDOW):
        @pl.when(c < j)
        def _():
            kbuf[j] = jnp.zeros(kbuf.shape[1:], kbuf.dtype)
            vbuf[j] = jnp.zeros(vbuf.shape[1:], vbuf.dtype)

    local[2].wait()
    clips[s] = jnp.broadcast_to(own_clip[...], clips.shape[1:])
    local[0].wait()
    local[1].wait()
    later_spans = jnp.minimum(spans - 1 - c, WINDOW - 1)
    z_neighbours = jnp.minimum(me, 1) + jnp.minimum(n - 1 - me, 1)
    pl.semaphore_wait(barrier, seqs - 1 + later_spans + z_neighbours)

    bufs = (kbuf, vbuf)

    def to_span(j, a):
        return pltpu.make_async_remote_copy(
            src_ref=bufs[a].at[0, s],
            dst_ref=bufs[a].at[j, s],
            send_sem=span_send.at[j, a],
            recv_sem=kv_recv.at[j, s, a],
            device_id={"span": c + j},
            device_id_type=MESH,
        )

    def to_seq(j, d, a):
        return pltpu.make_async_remote_copy(
            src_ref=bufs[a].at[j, s],
            dst_ref=bufs[a].at[j, s],
            send_sem=seq_send.at[j, d, a],
            recv_sem=kv_recv.at[j, s, a],
            device_id={"seq": lax.rem(s + d, seqs)},
            device_id_type=MESH,
        )

    def arrival(j, s2, a):
        return pltpu.make_async_remote_copy(
            src_ref=bufs[a].at[j, s2],
            dst_ref=bufs[a].at[j, s2],
            send_sem=seq_send.at[0, 0, a],
            recv_sem=kv_recv.at[j, s2, a],
            device_id={"seq": s2},
            device_id_type=MESH,
        )

    def clip_copy(d, source):
        return pltpu.make_async_remote_copy(
            src_ref=clips.at[source],
            dst_ref=clips.at[source],
            send_sem=clip_send.at[d],
            recv_sem=clip_recv.at[source],
            device_id={"seq": lax.rem(s + d, seqs)},
            device_id_type=MESH,
        )

    for a in range(2):
        for j in range(WINDOW - 1, 0, -1):
            @pl.when(c + j < spans)
            def _():
                to_span(j, a).start()
    for d in range(1, seqs):
        clip_copy(d, s).start()
    for a in range(2):
        for d in range(1, seqs):
            to_seq(0, d, a).start()

    def relay(a):
        for j in range(1, WINDOW):
            @pl.when(c >= j)
            def _():
                arrival(j, s, a).wait_recv()
                for d in range(1, seqs):
                    to_seq(j, d, a).start()

    def await_others(a):
        for d in range(1, seqs):
            arrival(0, lax.rem(s + d, seqs), a).wait_recv()
        for j in range(1, WINDOW):
            @pl.when(c >= j)
            def _():
                for d in range(1, seqs):
                    arrival(j, lax.rem(s + d, seqs), a).wait_recv()

    for d in range(1, seqs):
        clip_copy(d, lax.rem(s + d, seqs)).wait_recv()
    own = jnp.broadcast_to(own_clip[...], (rows, rows)).astype(jnp.float32)
    own_column = own.T
    same = [
        jnp.broadcast_to(clips[s2, 0:1, :], (rows, rows)).astype(jnp.float32) == own_column
        for s2 in range(seqs)
    ]
    local[4].wait()
    blocks = []
    for j in range(WINDOW):
        entry = mask[c, jnp.maximum(c - j, 0)]
        seen = jnp.where((c >= j) & (entry == 1), 0.0, MASKED).astype(jnp.float32)
        for s2 in range(seqs):
            blocks.append(jnp.where(same[s2], seen, MASKED))
    bias = jnp.concatenate(blocks, axis=1)

    local[3].wait()
    relay(0)
    relay(1)
    await_others(0)

    scale = HEAD_DIM ** (-0.5)
    key_count = WINDOW * seqs * rows
    stacked = GROUP if head_count % GROUP == 0 else 1
    probabilities = []
    for h in range(0, head_count, stacked):
        if head_count % GROUP == 0:
            g = h // GROUP
            keys = kbuf[:, :, :, g * HEAD_DIM:(g + 1) * HEAD_DIM]
        else:
            at = (me * head_count + h) // GROUP - first_kv
            keys = kbuf[:, :, :, 0:HEAD_DIM]
            for g in range(1, kv_count):
                keys = jnp.where(at == g, kbuf[:, :, :, g * HEAD_DIM:(g + 1) * HEAD_DIM], keys)
        keys = keys.reshape(key_count, HEAD_DIM)
        q = jnp.concatenate(
            [qbuf[:, i * HEAD_DIM:(i + 1) * HEAD_DIM] for i in range(h, h + stacked)], axis=0
        )
        scores = lax.dot_general(
            q, keys, (((1,), (1,)), ((), ())), preferred_element_type=jnp.float32
        ) * scale
        scores = scores.reshape(stacked, rows, key_count) + bias[None]
        top = jnp.max(scores, axis=2, keepdims=True)
        p = jnp.exp(scores - top)
        total = jnp.sum(p, axis=2, keepdims=True)
        probabilities.append((
            p.astype(jnp.bfloat16).reshape(stacked * rows, key_count),
            total.reshape(stacked * rows, 1),
        ))
    att_heads = GROUP if head_count % GROUP == 0 else head_count
    att_parts = head_count // att_heads

    def att_copy(i, source):
        columns = pl.ds(i * att_heads * HEAD_DIM, att_heads * HEAD_DIM)
        return pltpu.make_async_remote_copy(
            src_ref=att.at[source, :, columns],
            dst_ref=att.at[source, :, columns],
            send_sem=att_send.at[i],
            recv_sem=att_recv.at[i],
            device_id=sibling,
            device_id_type=MESH,
        )

    await_others(1)
    for h, (p, total) in zip(range(0, head_count, stacked), probabilities):
        if head_count % GROUP == 0:
            g = h // GROUP
            values = vbuf[:, :, :, g * HEAD_DIM:(g + 1) * HEAD_DIM]
        else:
            at = (me * head_count + h) // GROUP - first_kv
            values = vbuf[:, :, :, 0:HEAD_DIM]
            for g in range(1, kv_count):
                values = jnp.where(at == g, vbuf[:, :, :, g * HEAD_DIM:(g + 1) * HEAD_DIM], values)
        values = values.reshape(key_count, HEAD_DIM)
        o = jnp.dot(p, values, preferred_element_type=jnp.float32) / total
        o = o.astype(jnp.bfloat16)
        for i in range(stacked):
            att[core, :, (h + i) * HEAD_DIM:(h + i + 1) * HEAD_DIM] = o[i * rows:(i + 1) * rows]
        if (h + stacked) % att_heads == 0:
            att_copy((h + stacked) // att_heads - 1, core).start()
    for i in range(att_parts):
        att_copy(i, 1 - core).wait_recv()

    def pass_on(way, at):
        return pltpu.make_async_remote_copy(
            src_ref=sendbuf.at[at],
            dst_ref=recvbuf.at[way, at],
            send_sem=sum_send.at[at],
            recv_sem=sum_recv.at[way, at],
            device_id={"mp": me + 1 - 2 * way},
            device_id_type=MESH,
        )

    def project(i):
        to, piece = piece_at(i)
        at = to * pieces + piece
        w_copy(i).wait()
        product = jnp.dot(
            att[...].reshape(2 * rows, local_width), wbuf[i], preferred_element_type=jnp.float32
        )
        part[at] = product

        @pl.when((me == 0) & (to > 0))
        def _():
            sendbuf[at] = product.astype(sendbuf.dtype)
            pass_on(0, at).start()

        @pl.when((me == n - 1) & (to < n - 1))
        def _():
            sendbuf[at] = product.astype(sendbuf.dtype)
            pass_on(1, at).start()

    up_lag = 2 * me - 1
    down_lag = 2 * (n - 1 - me) - 1

    def relay_sums(m):
        up = (n - 1) * pieces - jnp.maximum(m - up_lag, 0) // pieces * pieces + lax.rem(
            jnp.maximum(m - up_lag, 0), pieces
        )

        @pl.when((me > 0) & (m >= up_lag) & (m - up_lag < up_count))
        def _():
            pass_on(0, up).wait_recv()
            sendbuf[up] = (part[up] + recvbuf[0, up].astype(jnp.float32)).astype(sendbuf.dtype)
            pass_on(0, up).start()

        down = jnp.maximum(m - down_lag, 0)

        @pl.when((me < n - 1) & (m >= down_lag) & (m - down_lag < down_count))
        def _():
            pass_on(1, down).wait_recv()
            sendbuf[down] = (part[down] + recvbuf[1, down].astype(jnp.float32)).astype(sendbuf.dtype)
            pass_on(1, down).start()

    def project_and_relay(m, carry):
        project(2 * m)
        project(2 * m + 1)
        relay_sums(m)
        return carry

    def relay_only(m, carry):
        relay_sums(m)
        return carry

    lax.fori_loop(0, steps // 2, project_and_relay, 0)
    last = max((n - 1 - z) * pieces + 2 * z - 1 for z in range(1, n))
    lax.fori_loop(steps // 2, last, relay_only, 0)

    def out_columns(i, of):
        return pl.ds(pl.multiple_of(of * half + i * width, HEAD_DIM), width)

    def out_copy(i):
        return pltpu.make_async_copy(
            outbuf.at[i, pl.ds(pl.multiple_of(core * rows, rows), rows)],
            out_ref.at[0, :, out_columns(i, core)],
            out_sem.at[i],
        )

    def out_to_sibling(i, of):
        return pltpu.make_async_remote_copy(
            src_ref=outbuf.at[i, pl.ds(pl.multiple_of((1 - core) * rows, rows), rows)],
            dst_ref=out_ref.at[0, :, out_columns(i, of)],
            send_sem=out_send.at[i],
            recv_sem=out_recv.at[i],
            device_id=sibling,
            device_id_type=MESH,
        )

    for i in range(pieces):
        at = me * pieces + i

        @pl.when(me > 0)
        def _():
            pass_on(0, at).wait_recv()
            part[at] += recvbuf[0, at].astype(jnp.float32)

        @pl.when(me < n - 1)
        def _():
            pass_on(1, at).wait_recv()
            part[at] += recvbuf[1, at].astype(jnp.float32)

        outbuf[i] = part[at].astype(outbuf.dtype)
        out_to_sibling(i, core).start()
        out_copy(i).start()

    for a in range(2):
        for j in range(1, WINDOW):
            @pl.when(c + j < spans)
            def _():
                to_span(j, a).wait_send()
            @pl.when(c >= j)
            def _():
                for d in range(1, seqs):
                    to_seq(j, d, a).wait_send()
        for d in range(1, seqs):
            to_seq(0, d, a).wait_send()
    for d in range(1, seqs):
        clip_copy(d, s).wait_send()

    def sent(i, carry):
        @pl.when(i // pieces != me)
        def _():
            pass_on(0, i).wait_send()

        return carry

    lax.fori_loop(0, steps, sent, 0)
    for i in range(att_parts):
        att_copy(i, core).wait_send()
    for i in range(pieces):
        out_copy(i).wait()
        out_to_sibling(i, core).wait_send()
        out_to_sibling(i, 1 - core).wait_recv()


def on_device(queries, keys, values, clip_ids, block_mask, out_weight):
    spans = lax.axis_size("span")
    seqs = lax.axis_size("seq")
    n = lax.axis_size("mp")
    _, rows, local_width = queries.shape
    head_count = local_width // HEAD_DIM
    kv_total = keys.shape[2] // HEAD_DIM
    firsts = [m * head_count // GROUP for m in range(n)]
    lasts = [((m + 1) * head_count - 1) // GROUP for m in range(n)]
    kv_count = max(b - a + 1 for a, b in zip(firsts, lasts))
    kv_width = kv_count * HEAD_DIM
    depth, out_width = out_weight.shape
    chunk = out_width // n
    width = 256 if chunk % 512 == 0 else HEAD_DIM
    pieces = chunk // 2 // width
    bf16 = jnp.bfloat16
    hbm = pl.BlockSpec(memory_space=pl.ANY)
    return pl.pallas_call(
        functools.partial(kernel, spans, seqs, n, pieces, kv_count, kv_total),
        out_shape=jax.ShapeDtypeStruct((1, rows, chunk), bf16),
        in_specs=[hbm] * 6,
        out_specs=hbm,
        scratch_shapes=[
            pltpu.VMEM((rows, local_width), bf16),
            pltpu.VMEM((WINDOW, seqs, rows, kv_width), bf16),
            pltpu.VMEM((WINDOW, seqs, rows, kv_width), bf16),
            pltpu.VMEM((1, rows), jnp.int32),
            pltpu.SMEM(block_mask.shape, jnp.int32),
            pltpu.VMEM((seqs, 8, rows), jnp.int32),
            pltpu.VMEM((n * pieces, depth, width), bf16),
            pltpu.VMEM((2, rows, local_width), bf16),
            pltpu.VMEM((n * pieces, 2 * rows, width), jnp.float32),
            pltpu.VMEM((n * pieces, 2 * rows, width), bf16),
            pltpu.VMEM((2, n * pieces, 2 * rows, width), bf16),
            pltpu.VMEM((pieces, 2 * rows, width), bf16),
            pltpu.SemaphoreType.DMA((5,)),
            pltpu.SemaphoreType.DMA((n * pieces,)),
            pltpu.SemaphoreType.DMA((WINDOW, 2)),
            pltpu.SemaphoreType.DMA((WINDOW, seqs, 2)),
            pltpu.SemaphoreType.DMA((WINDOW, seqs, 2)),
            pltpu.SemaphoreType.DMA((seqs,)),
            pltpu.SemaphoreType.DMA((seqs,)),
            pltpu.SemaphoreType.DMA((n * pieces,)),
            pltpu.SemaphoreType.DMA((2, n * pieces)),
            pltpu.SemaphoreType.DMA((pieces,)),
            pltpu.SemaphoreType.DMA((local_width // HEAD_DIM,)),
            pltpu.SemaphoreType.DMA((local_width // HEAD_DIM,)),
            pltpu.SemaphoreType.DMA((pieces,)),
            pltpu.SemaphoreType.DMA((pieces,)),
        ],
        compiler_params=pltpu.CompilerParams(
            collective_id=0, has_side_effects=True, vmem_limit_bytes=64 * 1024 * 1024
        ),
    )(queries, keys, values, clip_ids.reshape(1, rows), block_mask, out_weight)


def solution(mesh):
    in_specs = (
        P("span", "seq", "mp"),
        P("span", "seq", None),
        P("span", "seq", None),
        P("seq"),
        P(),
        P("mp", None),
    )
    out_specs = P("span", "seq", "mp")
    return jax.shard_map(
        on_device, mesh=mesh, in_specs=in_specs, out_specs=out_specs, check_vma=False
    )
```

```python
import functools
import math
import jax
import jax.numpy as jnp
from jax import lax
from jax.experimental import pallas as pl
from jax.experimental.pallas import tpu as pltpu
from jax.sharding import PartitionSpec as P

HEAD_DIM = 128
WINDOW = 3
GROUP = 6
MASKED = -1e30
MESH = pl.DeviceIdType.MESH


def kernel(
    spans, seqs, n, pieces,
    q_ref, k_ref, v_ref, clip_ref, mask_ref, w_ref, out_ref,
    qbuf, q_other, kbuf, vbuf, other, own_clip, mask, clips, wbuf, att, part, sendbuf, recvbuf, outbuf,
    local_sem, w_sem, q_sem, kv_send, kv_recv, clip_send, clip_recv, sum_send, sum_recv, out_sem,
    att_send, att_recv, out_send, out_recv,
):
    _, rows, local_width = q_ref.shape
    head_count = local_width // HEAD_DIM
    width = wbuf.shape[2]
    half = width * pieces
    steps = n * pieces
    c = lax.axis_index("span")
    s = lax.axis_index("seq")
    me = lax.axis_index("mp")
    core = lax.rem(s, 2)
    sibling = {"seq": s + 1 - 2 * core}

    my_heads = head_count // 2
    buddy = s + 1 - 2 * core

    def kv_columns(of):
        group = (me * head_count + of * my_heads) // GROUP
        return pl.ds(pl.multiple_of(group * HEAD_DIM, HEAD_DIM), HEAD_DIM)

    def q_columns(of):
        return pl.ds(pl.multiple_of(of * my_heads * HEAD_DIM, HEAD_DIM), my_heads * HEAD_DIM)

    local = [
        pltpu.make_async_copy(k_ref.at[0, :, kv_columns(core)], kbuf.at[0, s], local_sem.at[0]),
        pltpu.make_async_copy(k_ref.at[0, :, kv_columns(1 - core)], other.at[0], local_sem.at[1]),
        pltpu.make_async_copy(q_ref.at[0, :, q_columns(1 - core)], q_other, local_sem.at[2]),
        pltpu.make_async_copy(v_ref.at[0, :, kv_columns(core)], vbuf.at[0, s], local_sem.at[3]),
        pltpu.make_async_copy(v_ref.at[0, :, kv_columns(1 - core)], other.at[1], local_sem.at[4]),
        pltpu.make_async_copy(clip_ref, own_clip, local_sem.at[5]),
        pltpu.make_async_copy(mask_ref, mask, local_sem.at[6]),
        pltpu.make_async_copy(q_ref.at[0, :, q_columns(core)], qbuf.at[core], local_sem.at[7]),
    ]
    for copy in local:
        copy.start()

    up_count = (n - 1 - me) * pieces
    down_count = me * pieces
    both = jnp.minimum(up_count, down_count)

    def piece_at(i):
        k = jnp.where(i < 2 * both, i // 2, i - both)
        goes_up = jnp.where(i < 2 * both, 1 - lax.rem(i, 2), jnp.where(up_count > down_count, 1, 0))
        moving = jnp.where(goes_up == 1, n - 1 - k // pieces, k // pieces)
        to = jnp.where(i < up_count + down_count, moving, me)
        return to, lax.rem(k, pieces)

    def w_copy(i):
        to, piece = piece_at(i)
        start = (to * 2 + core) * half + piece * width
        return pltpu.make_async_copy(
            w_ref.at[:, pl.ds(pl.multiple_of(start, HEAD_DIM), width)], wbuf.at[i], w_sem.at[i]
        )

    barrier = pltpu.get_barrier_semaphore()
    for j in range(1, WINDOW):
        @pl.when(c >= j)
        def _():
            for s2 in range(seqs):
                pl.semaphore_signal(
                    barrier, inc=1, device_id={"span": c - j, "seq": s2}, device_id_type=MESH
                )
    for d in range(1, seqs):
        pl.semaphore_signal(
            barrier, inc=1, device_id={"seq": lax.rem(s + d, seqs)}, device_id_type=MESH
        )

    @pl.when(me > 0)
    def _():
        pl.semaphore_signal(barrier, inc=1, device_id={"mp": me - 1}, device_id_type=MESH)

    @pl.when(me < n - 1)
    def _():
        pl.semaphore_signal(barrier, inc=1, device_id={"mp": me + 1}, device_id_type=MESH)

    def start_w(i, carry):
        w_copy(i).start()
        return carry

    lax.fori_loop(0, steps, start_w, 0)

    for j in range(1, WINDOW):
        @pl.when(c < j)
        def _():
            kbuf[j] = jnp.zeros(kbuf.shape[1:], kbuf.dtype)
            vbuf[j] = jnp.zeros(vbuf.shape[1:], vbuf.dtype)

    local[5].wait()
    clips[s] = jnp.broadcast_to(own_clip[...], clips.shape[1:])
    for i in range(5):
        local[i].wait()
    later_spans = jnp.minimum(spans - 1 - c, WINDOW - 1)
    z_neighbours = jnp.minimum(me, 1) + jnp.minimum(n - 1 - me, 1)
    pl.semaphore_wait(barrier, seqs - 1 + seqs * later_spans + z_neighbours)

    bufs = (kbuf, vbuf)

    def kv_copy(j, d, a):
        source = bufs[a].at[0, s] if d % 2 == 0 else other.at[a]
        return pltpu.make_async_remote_copy(
            src_ref=source,
            dst_ref=bufs[a].at[j, s],
            send_sem=kv_send.at[j, d, a],
            recv_sem=kv_recv.at[j, s, a],
            device_id={"span": c + j, "seq": lax.rem(s + d, seqs)},
            device_id_type=MESH,
        )

    def arrival(j, s2, a):
        return pltpu.make_async_remote_copy(
            src_ref=bufs[a].at[j, s2],
            dst_ref=bufs[a].at[j, s2],
            send_sem=kv_send.at[0, 0, a],
            recv_sem=kv_recv.at[j, s2, a],
            device_id={"seq": buddy},
            device_id_type=MESH,
        )

    def clip_copy(d, source):
        return pltpu.make_async_remote_copy(
            src_ref=clips.at[source],
            dst_ref=clips.at[source],
            send_sem=clip_send.at[d],
            recv_sem=clip_recv.at[source],
            device_id={"seq": lax.rem(s + d, seqs)},
            device_id_type=MESH,
        )

    def q_copy(at):
        return pltpu.make_async_remote_copy(
            src_ref=q_other,
            dst_ref=qbuf.at[at],
            send_sem=q_sem.at[0],
            recv_sem=q_sem.at[1],
            device_id=sibling,
            device_id_type=MESH,
        )

    for a in range(2):
        for j in range(WINDOW - 1, 0, -1):
            @pl.when(c + j < spans)
            def _():
                for d in range(seqs):
                    kv_copy(j, d, a).start()
        for d in range(1, seqs):
            kv_copy(0, d, a).start()
        if a == 0:
            q_copy(core).start()
            for d in range(1, seqs):
                clip_copy(d, s).start()

    def await_block(j, a):
        if j == 0:
            for d in range(1, seqs):
                arrival(0, lax.rem(s + d, seqs), a).wait_recv()
        else:
            @pl.when(c >= j)
            def _():
                for s2 in range(seqs):
                    arrival(j, s2, a).wait_recv()

    for d in range(1, seqs):
        clip_copy(d, lax.rem(s + d, seqs)).wait_recv()
    local[6].wait()

    def clip_square(s2):
        return jnp.broadcast_to(clips[s2, 0:1, :], (rows, rows)).astype(jnp.float32)

    columns = [clip_square(s - core + r).T for r in range(2)]
    same = [[clip_square(s2) == column for s2 in range(seqs)] for column in columns]

    local[7].wait()
    q_copy(1 - core).wait_recv()
    queries = jnp.concatenate(
        [
            qbuf[:, :, i * HEAD_DIM:(i + 1) * HEAD_DIM].reshape(2 * rows, HEAD_DIM)
            for i in range(my_heads)
        ],
        axis=0,
    )
    piece = seqs * rows
    scores = []
    for j in range(WINDOW):
        entry = mask[c, jnp.maximum(c - j, 0)]
        seen = jnp.where((c >= j) & (entry == 1), 0.0, MASKED).astype(jnp.float32)
        bias = jnp.concatenate(
            [
                jnp.concatenate([jnp.where(same[r][s2], seen, MASKED) for s2 in range(seqs)], axis=1)
                for r in range(2)
            ],
            axis=0,
        )
        await_block(j, 0)
        dots = lax.dot_general(
            queries, kbuf[j].reshape(piece, HEAD_DIM), (((1,), (1,)), ((), ())),
            preferred_element_type=jnp.float32,
        )
        scores.append(dots.reshape(my_heads, 2 * rows, piece) + bias[None])
    scores = jnp.concatenate(scores, axis=2)
    top = jnp.max(scores, axis=2, keepdims=True)
    scale = HEAD_DIM ** (-0.5) * math.log2(math.e)
    weights = jnp.exp2((scores - top) * scale).astype(jnp.bfloat16)
    for j in range(WINDOW):
        await_block(j, 1)
    key_count = WINDOW * piece
    values = jnp.concatenate(
        [vbuf[...].reshape(key_count, HEAD_DIM), jnp.ones((key_count, HEAD_DIM), jnp.bfloat16)],
        axis=1,
    )

    att_parts = 2
    att_heads = my_heads // att_parts

    def att_copy(i, source):
        part_columns = pl.ds(i * att_heads * HEAD_DIM, att_heads * HEAD_DIM)
        return pltpu.make_async_remote_copy(
            src_ref=att.at[source, :, part_columns],
            dst_ref=att.at[source, :, part_columns],
            send_sem=att_send.at[i],
            recv_sem=att_recv.at[i],
            device_id=sibling,
            device_id_type=MESH,
        )

    for i in range(att_parts):
        heads = slice(i * att_heads, (i + 1) * att_heads)
        both_sums = jnp.dot(
            weights[heads].reshape(att_heads * 2 * rows, key_count), values,
            preferred_element_type=jnp.float32,
        )
        o = (both_sums[:, :HEAD_DIM] / both_sums[:, HEAD_DIM:]).astype(jnp.bfloat16)
        for h in range(att_heads):
            at = (i * att_heads + h) * HEAD_DIM
            att[core, :, at:at + HEAD_DIM] = o[h * 2 * rows:(h + 1) * 2 * rows]
        att_copy(i, core).start()
    for i in range(att_parts):
        att_copy(i, 1 - core).wait_recv()

    def pass_on(way, at):
        return pltpu.make_async_remote_copy(
            src_ref=sendbuf.at[at],
            dst_ref=recvbuf.at[way, at],
            send_sem=sum_send.at[at],
            recv_sem=sum_recv.at[way, at],
            device_id={"mp": me + 1 - 2 * way},
            device_id_type=MESH,
        )

    def project(i):
        to, piece = piece_at(i)
        at = to * pieces + piece
        w_copy(i).wait()
        product = jnp.dot(
            jnp.concatenate([att[0], att[1]], axis=1), wbuf[i], preferred_element_type=jnp.float32
        )
        part[at] = product

        @pl.when((me == 0) & (to > 0))
        def _():
            sendbuf[at] = product.astype(sendbuf.dtype)
            pass_on(0, at).start()

        @pl.when((me == n - 1) & (to < n - 1))
        def _():
            sendbuf[at] = product.astype(sendbuf.dtype)
            pass_on(1, at).start()

    up_lag = 2 * me - 1
    down_lag = 2 * (n - 1 - me) - 1

    def relay_sums(m):
        up = (n - 1) * pieces - jnp.maximum(m - up_lag, 0) // pieces * pieces + lax.rem(
            jnp.maximum(m - up_lag, 0), pieces
        )

        @pl.when((me > 0) & (m >= up_lag) & (m - up_lag < up_count))
        def _():
            pass_on(0, up).wait_recv()
            sendbuf[up] = (part[up] + recvbuf[0, up].astype(jnp.float32)).astype(sendbuf.dtype)
            pass_on(0, up).start()

        down = jnp.maximum(m - down_lag, 0)

        @pl.when((me < n - 1) & (m >= down_lag) & (m - down_lag < down_count))
        def _():
            pass_on(1, down).wait_recv()
            sendbuf[down] = (part[down] + recvbuf[1, down].astype(jnp.float32)).astype(sendbuf.dtype)
            pass_on(1, down).start()

    def project_and_relay(m, carry):
        project(2 * m)
        project(2 * m + 1)
        relay_sums(m)
        return carry

    def relay_only(m, carry):
        relay_sums(m)
        return carry

    lax.fori_loop(0, steps // 2, project_and_relay, 0)
    last = max((n - 1 - z) * pieces + 2 * z - 1 for z in range(1, n))
    lax.fori_loop(steps // 2, last, relay_only, 0)

    def out_columns(i, of):
        return pl.ds(pl.multiple_of(of * half + i * width, HEAD_DIM), width)

    def out_copy(i):
        return pltpu.make_async_copy(
            outbuf.at[i, pl.ds(pl.multiple_of(core * rows, rows), rows)],
            out_ref.at[0, :, out_columns(i, core)],
            out_sem.at[i],
        )

    def out_to_sibling(i, of):
        return pltpu.make_async_remote_copy(
            src_ref=outbuf.at[i, pl.ds(pl.multiple_of((1 - core) * rows, rows), rows)],
            dst_ref=out_ref.at[0, :, out_columns(i, of)],
            send_sem=out_send.at[i],
            recv_sem=out_recv.at[i],
            device_id=sibling,
            device_id_type=MESH,
        )

    for i in range(pieces):
        at = me * pieces + i

        @pl.when(me > 0)
        def _():
            pass_on(0, at).wait_recv()
            part[at] += recvbuf[0, at].astype(jnp.float32)

        @pl.when(me < n - 1)
        def _():
            pass_on(1, at).wait_recv()
            part[at] += recvbuf[1, at].astype(jnp.float32)

        outbuf[i] = part[at].astype(outbuf.dtype)
        out_to_sibling(i, core).start()
        out_copy(i).start()

    for a in range(2):
        for j in range(1, WINDOW):
            @pl.when(c + j < spans)
            def _():
                for d in range(seqs):
                    kv_copy(j, d, a).wait_send()
        for d in range(1, seqs):
            kv_copy(0, d, a).wait_send()
    q_copy(core).wait_send()
    for d in range(1, seqs):
        clip_copy(d, s).wait_send()

    def sent(i, carry):
        @pl.when(i // pieces != me)
        def _():
            pass_on(0, i).wait_send()

        return carry

    lax.fori_loop(0, steps, sent, 0)
    for i in range(att_parts):
        att_copy(i, core).wait_send()
    for i in range(pieces):
        out_copy(i).wait()
        out_to_sibling(i, core).wait_send()
        out_to_sibling(i, 1 - core).wait_recv()


def on_device(queries, keys, values, clip_ids, block_mask, out_weight):
    spans = lax.axis_size("span")
    seqs = lax.axis_size("seq")
    n = lax.axis_size("mp")
    _, rows, local_width = queries.shape
    assert GROUP % (local_width // HEAD_DIM // 2) == 0
    depth, out_width = out_weight.shape
    chunk = out_width // n
    width = 256 if chunk % 512 == 0 else HEAD_DIM
    pieces = chunk // 2 // width
    bf16 = jnp.bfloat16
    hbm = pl.BlockSpec(memory_space=pl.ANY)
    return pl.pallas_call(
        functools.partial(kernel, spans, seqs, n, pieces),
        out_shape=jax.ShapeDtypeStruct((1, rows, chunk), bf16),
        in_specs=[hbm] * 6,
        out_specs=hbm,
        scratch_shapes=[
            pltpu.VMEM((2, rows, local_width // 2), bf16),
            pltpu.VMEM((rows, local_width // 2), bf16),
            pltpu.VMEM((WINDOW, seqs, rows, HEAD_DIM), bf16),
            pltpu.VMEM((WINDOW, seqs, rows, HEAD_DIM), bf16),
            pltpu.VMEM((2, rows, HEAD_DIM), bf16),
            pltpu.VMEM((1, rows), jnp.int32),
            pltpu.SMEM(block_mask.shape, jnp.int32),
            pltpu.VMEM((seqs, 8, rows), jnp.int32),
            pltpu.VMEM((n * pieces, depth, width), bf16),
            pltpu.VMEM((2, 2 * rows, local_width // 2), bf16),
            pltpu.VMEM((n * pieces, 2 * rows, width), jnp.float32),
            pltpu.VMEM((n * pieces, 2 * rows, width), bf16),
            pltpu.VMEM((2, n * pieces, 2 * rows, width), bf16),
            pltpu.VMEM((pieces, 2 * rows, width), bf16),
            pltpu.SemaphoreType.DMA((8,)),
            pltpu.SemaphoreType.DMA((n * pieces,)),
            pltpu.SemaphoreType.DMA((2,)),
            pltpu.SemaphoreType.DMA((WINDOW, seqs, 2)),
            pltpu.SemaphoreType.DMA((WINDOW, seqs, 2)),
            pltpu.SemaphoreType.DMA((seqs,)),
            pltpu.SemaphoreType.DMA((seqs,)),
            pltpu.SemaphoreType.DMA((n * pieces,)),
            pltpu.SemaphoreType.DMA((2, n * pieces)),
            pltpu.SemaphoreType.DMA((pieces,)),
            pltpu.SemaphoreType.DMA((2,)),
            pltpu.SemaphoreType.DMA((2,)),
            pltpu.SemaphoreType.DMA((pieces,)),
            pltpu.SemaphoreType.DMA((pieces,)),
        ],
        compiler_params=pltpu.CompilerParams(
            collective_id=0, has_side_effects=True, vmem_limit_bytes=64 * 1024 * 1024
        ),
    )(queries, keys, values, clip_ids.reshape(1, rows), block_mask, out_weight)


def solution(mesh):
    in_specs = (
        P("span", "seq", "mp"),
        P("span", "seq", None),
        P("span", "seq", None),
        P("seq"),
        P(),
        P("mp", None),
    )
    out_specs = P("span", "seq", "mp")
    return jax.shard_map(
        on_device, mesh=mesh, in_specs=in_specs, out_specs=out_specs, check_vma=False
    )
```

```python
import functools
import math
import jax
import jax.numpy as jnp
from jax import lax
from jax.experimental import pallas as pl
from jax.experimental.pallas import tpu as pltpu
from jax.sharding import PartitionSpec as P

HEAD_DIM = 128
WINDOW = 3
GROUP = 6
MASKED = -1e30
MESH = pl.DeviceIdType.MESH


def kernel(
    spans, seqs, n, pieces,
    q_ref, k_ref, v_ref, clip_ref, mask_ref, w_ref, out_ref,
    qbuf, q_other, kbuf, vbuf, other, own_clip, mask, clips, wbuf, att, part, sendbuf, recvbuf, outbuf,
    local_sem, w_sem, q_sem, kv_send, kv_recv, clip_send, clip_recv, sum_send, sum_recv, out_sem,
    att_send, att_recv, out_send, out_recv,
):
    _, rows, local_width = q_ref.shape
    head_count = local_width // HEAD_DIM
    width = wbuf.shape[2]
    half = width * pieces
    steps = n * pieces
    c = lax.axis_index("span")
    s = lax.axis_index("seq")
    me = lax.axis_index("mp")
    core = lax.rem(s, 2)
    sibling = {"seq": s + 1 - 2 * core}

    barrier = pltpu.get_barrier_semaphore()
    for j in range(1, WINDOW):
        @pl.when(c >= j)
        def _():
            for s2 in range(seqs):
                pl.semaphore_signal(
                    barrier, inc=1, device_id={"span": c - j, "seq": s2}, device_id_type=MESH
                )
    for d in range(1, seqs):
        pl.semaphore_signal(
            barrier, inc=1, device_id={"seq": lax.rem(s + d, seqs)}, device_id_type=MESH
        )

    @pl.when(me > 0)
    def _():
        pl.semaphore_signal(barrier, inc=1, device_id={"mp": me - 1}, device_id_type=MESH)

    @pl.when(me < n - 1)
    def _():
        pl.semaphore_signal(barrier, inc=1, device_id={"mp": me + 1}, device_id_type=MESH)

    my_heads = head_count // 2
    buddy = s + 1 - 2 * core

    def kv_columns(of):
        group = (me * head_count + of * my_heads) // GROUP
        return pl.ds(pl.multiple_of(group * HEAD_DIM, HEAD_DIM), HEAD_DIM)

    def q_columns(of):
        return pl.ds(pl.multiple_of(of * my_heads * HEAD_DIM, HEAD_DIM), my_heads * HEAD_DIM)

    local = [
        pltpu.make_async_copy(k_ref.at[0, :, kv_columns(core)], kbuf.at[0, s], local_sem.at[0]),
        pltpu.make_async_copy(k_ref.at[0, :, kv_columns(1 - core)], other.at[0], local_sem.at[1]),
        pltpu.make_async_copy(q_ref.at[0, :, q_columns(1 - core)], q_other, local_sem.at[2]),
        pltpu.make_async_copy(v_ref.at[0, :, kv_columns(core)], vbuf.at[0, s], local_sem.at[3]),
        pltpu.make_async_copy(v_ref.at[0, :, kv_columns(1 - core)], other.at[1], local_sem.at[4]),
        pltpu.make_async_copy(clip_ref, own_clip, local_sem.at[5]),
        pltpu.make_async_copy(mask_ref, mask, local_sem.at[6]),
        pltpu.make_async_copy(q_ref.at[0, :, q_columns(core)], qbuf.at[core], local_sem.at[7]),
    ]
    for copy in local:
        copy.start()

    up_count = (n - 1 - me) * pieces
    down_count = me * pieces
    both = jnp.minimum(up_count, down_count)

    def piece_at(i):
        k = jnp.where(i < 2 * both, i // 2, i - both)
        goes_up = jnp.where(i < 2 * both, 1 - lax.rem(i, 2), jnp.where(up_count > down_count, 1, 0))
        moving = jnp.where(goes_up == 1, n - 1 - k // pieces, k // pieces)
        to = jnp.where(i < up_count + down_count, moving, me)
        return to, lax.rem(k, pieces)

    def w_copy(i):
        to, piece = piece_at(i)
        start = (to * 2 + core) * half + piece * width
        return pltpu.make_async_copy(
            w_ref.at[:, pl.ds(pl.multiple_of(start, HEAD_DIM), width)], wbuf.at[i], w_sem.at[i]
        )

    for j in range(1, WINDOW):
        @pl.when(c < j)
        def _():
            kbuf[j] = jnp.zeros(kbuf.shape[1:], kbuf.dtype)
            vbuf[j] = jnp.zeros(vbuf.shape[1:], vbuf.dtype)

    local[5].wait()
    clips[s] = jnp.broadcast_to(own_clip[...], clips.shape[1:])
    for i in range(2):
        local[i].wait()
    later_spans = jnp.minimum(spans - 1 - c, WINDOW - 1)
    z_neighbours = jnp.minimum(me, 1) + jnp.minimum(n - 1 - me, 1)
    pl.semaphore_wait(barrier, seqs - 1 + seqs * later_spans + z_neighbours)

    bufs = (kbuf, vbuf)

    def kv_copy(j, d, a):
        source = bufs[a].at[0, s] if d % 2 == 0 else other.at[a]
        return pltpu.make_async_remote_copy(
            src_ref=source,
            dst_ref=bufs[a].at[j, s],
            send_sem=kv_send.at[j, d, a],
            recv_sem=kv_recv.at[j, s, a],
            device_id={"span": c + j, "seq": lax.rem(s + d, seqs)},
            device_id_type=MESH,
        )

    def arrival(j, s2, a):
        return pltpu.make_async_remote_copy(
            src_ref=bufs[a].at[j, s2],
            dst_ref=bufs[a].at[j, s2],
            send_sem=kv_send.at[0, 0, a],
            recv_sem=kv_recv.at[j, s2, a],
            device_id={"seq": buddy},
            device_id_type=MESH,
        )

    def clip_copy(d, source):
        return pltpu.make_async_remote_copy(
            src_ref=clips.at[source],
            dst_ref=clips.at[source],
            send_sem=clip_send.at[d],
            recv_sem=clip_recv.at[source],
            device_id={"seq": lax.rem(s + d, seqs)},
            device_id_type=MESH,
        )

    def q_copy(at):
        return pltpu.make_async_remote_copy(
            src_ref=q_other,
            dst_ref=qbuf.at[at],
            send_sem=q_sem.at[0],
            recv_sem=q_sem.at[1],
            device_id=sibling,
            device_id_type=MESH,
        )

    for a in range(2):
        for j in range(1, WINDOW):
            @pl.when(c + j < spans)
            def _():
                for d in range(seqs):
                    kv_copy(j, d, a).start()
        for d in range(1, seqs):
            kv_copy(0, d, a).start()
        if a == 0:
            local[2].wait()
            q_copy(core).start()
            for d in range(1, seqs):
                clip_copy(d, s).start()
            local[3].wait()
            local[4].wait()

    def start_w(i, carry):
        w_copy(i).start()
        return carry

    lax.fori_loop(0, steps, start_w, 0)

    def await_block(j, a):
        if j == 0:
            for d in range(1, seqs):
                arrival(0, lax.rem(s + d, seqs), a).wait_recv()
        else:
            @pl.when(c >= j)
            def _():
                for s2 in range(seqs):
                    arrival(j, s2, a).wait_recv()

    for d in range(1, seqs):
        clip_copy(d, lax.rem(s + d, seqs)).wait_recv()
    local[6].wait()

    def clip_square(s2):
        return jnp.broadcast_to(clips[s2, 0:1, :], (rows, rows)).astype(jnp.float32)

    columns = [clip_square(s - core + r).T for r in range(2)]
    same = [[clip_square(s2) == column for s2 in range(seqs)] for column in columns]

    local[7].wait()
    q_copy(1 - core).wait_recv()
    queries = jnp.concatenate(
        [
            qbuf[:, :, i * HEAD_DIM:(i + 1) * HEAD_DIM].reshape(2 * rows, HEAD_DIM)
            for i in range(my_heads)
        ],
        axis=0,
    )
    piece = seqs * rows
    scores = []
    for j in range(WINDOW):
        entry = mask[c, jnp.maximum(c - j, 0)]
        seen = jnp.where((c >= j) & (entry == 1), 0.0, MASKED).astype(jnp.float32)
        bias = jnp.concatenate(
            [
                jnp.concatenate([jnp.where(same[r][s2], seen, MASKED) for s2 in range(seqs)], axis=1)
                for r in range(2)
            ],
            axis=0,
        )
        await_block(j, 0)
        dots = lax.dot_general(
            queries, kbuf[j].reshape(piece, HEAD_DIM), (((1,), (1,)), ((), ())),
            preferred_element_type=jnp.float32,
        )
        scores.append(dots.reshape(my_heads, 2 * rows, piece) + bias[None])
    scores = jnp.concatenate(scores, axis=2)
    top = jnp.max(scores, axis=2, keepdims=True)
    scale = HEAD_DIM ** (-0.5) * math.log2(math.e)
    weights = jnp.exp2((scores - top) * scale).astype(jnp.bfloat16)
    for j in range(WINDOW):
        await_block(j, 1)
    key_count = WINDOW * piece
    values = jnp.concatenate(
        [vbuf[...].reshape(key_count, HEAD_DIM), jnp.ones((key_count, HEAD_DIM), jnp.bfloat16)],
        axis=1,
    )

    att_parts = 2
    att_heads = my_heads // att_parts

    def att_copy(i, source):
        part_columns = pl.ds(i * att_heads * HEAD_DIM, att_heads * HEAD_DIM)
        return pltpu.make_async_remote_copy(
            src_ref=att.at[source, :, part_columns],
            dst_ref=att.at[source, :, part_columns],
            send_sem=att_send.at[i],
            recv_sem=att_recv.at[i],
            device_id=sibling,
            device_id_type=MESH,
        )

    for i in range(att_parts):
        heads = slice(i * att_heads, (i + 1) * att_heads)
        both_sums = jnp.dot(
            weights[heads].reshape(att_heads * 2 * rows, key_count), values,
            preferred_element_type=jnp.float32,
        )
        o = (both_sums[:, :HEAD_DIM] / both_sums[:, HEAD_DIM:]).astype(jnp.bfloat16)
        for h in range(att_heads):
            at = (i * att_heads + h) * HEAD_DIM
            att[core, :, at:at + HEAD_DIM] = o[h * 2 * rows:(h + 1) * 2 * rows]
        att_copy(i, core).start()
    for i in range(att_parts):
        att_copy(i, 1 - core).wait_recv()

    def pass_on(way, at):
        return pltpu.make_async_remote_copy(
            src_ref=sendbuf.at[at],
            dst_ref=recvbuf.at[way, at],
            send_sem=sum_send.at[at],
            recv_sem=sum_recv.at[way, at],
            device_id={"mp": me + 1 - 2 * way},
            device_id_type=MESH,
        )

    def project(i):
        to, piece = piece_at(i)
        at = to * pieces + piece
        w_copy(i).wait()
        product = jnp.dot(
            jnp.concatenate([att[0], att[1]], axis=1), wbuf[i], preferred_element_type=jnp.float32
        )
        part[at] = product

        @pl.when((me == 0) & (to > 0))
        def _():
            sendbuf[at] = product.astype(sendbuf.dtype)
            pass_on(0, at).start()

        @pl.when((me == n - 1) & (to < n - 1))
        def _():
            sendbuf[at] = product.astype(sendbuf.dtype)
            pass_on(1, at).start()

    up_lag = 2 * me - 1
    down_lag = 2 * (n - 1 - me) - 1

    def relay_sums(m):
        up = (n - 1) * pieces - jnp.maximum(m - up_lag, 0) // pieces * pieces + lax.rem(
            jnp.maximum(m - up_lag, 0), pieces
        )

        @pl.when((me > 0) & (m >= up_lag) & (m - up_lag < up_count))
        def _():
            pass_on(0, up).wait_recv()
            sendbuf[up] = (part[up] + recvbuf[0, up].astype(jnp.float32)).astype(sendbuf.dtype)
            pass_on(0, up).start()

        down = jnp.maximum(m - down_lag, 0)

        @pl.when((me < n - 1) & (m >= down_lag) & (m - down_lag < down_count))
        def _():
            pass_on(1, down).wait_recv()
            sendbuf[down] = (part[down] + recvbuf[1, down].astype(jnp.float32)).astype(sendbuf.dtype)
            pass_on(1, down).start()

    def project_and_relay(m, carry):
        project(2 * m)
        project(2 * m + 1)
        relay_sums(m)
        return carry

    def relay_only(m, carry):
        relay_sums(m)
        return carry

    lax.fori_loop(0, steps // 2, project_and_relay, 0)
    last = max((n - 1 - z) * pieces + 2 * z - 1 for z in range(1, n))
    lax.fori_loop(steps // 2, last, relay_only, 0)

    def out_columns(i, of):
        return pl.ds(pl.multiple_of(of * half + i * width, HEAD_DIM), width)

    def out_copy(i):
        return pltpu.make_async_copy(
            outbuf.at[i, pl.ds(pl.multiple_of(core * rows, rows), rows)],
            out_ref.at[0, :, out_columns(i, core)],
            out_sem.at[i],
        )

    def out_to_sibling(i, of):
        return pltpu.make_async_remote_copy(
            src_ref=outbuf.at[i, pl.ds(pl.multiple_of((1 - core) * rows, rows), rows)],
            dst_ref=out_ref.at[0, :, out_columns(i, of)],
            send_sem=out_send.at[i],
            recv_sem=out_recv.at[i],
            device_id=sibling,
            device_id_type=MESH,
        )

    for i in range(pieces):
        at = me * pieces + i

        @pl.when(me > 0)
        def _():
            pass_on(0, at).wait_recv()
            part[at] += recvbuf[0, at].astype(jnp.float32)

        @pl.when(me < n - 1)
        def _():
            pass_on(1, at).wait_recv()
            part[at] += recvbuf[1, at].astype(jnp.float32)

        outbuf[i] = part[at]
        out_to_sibling(i, core).start()
        out_copy(i).start()

    for a in range(2):
        for j in range(1, WINDOW):
            @pl.when(c + j < spans)
            def _():
                for d in range(seqs):
                    kv_copy(j, d, a).wait_send()
        for d in range(1, seqs):
            kv_copy(0, d, a).wait_send()
    q_copy(core).wait_send()
    for d in range(1, seqs):
        clip_copy(d, s).wait_send()

    def sent(i, carry):
        @pl.when(i // pieces != me)
        def _():
            pass_on(0, i).wait_send()

        return carry

    lax.fori_loop(0, steps, sent, 0)
    for i in range(att_parts):
        att_copy(i, core).wait_send()
    for i in range(pieces):
        out_copy(i).wait()
        out_to_sibling(i, core).wait_send()
        out_to_sibling(i, 1 - core).wait_recv()


def on_device(queries, keys, values, clip_ids, block_mask, out_weight):
    spans = lax.axis_size("span")
    seqs = lax.axis_size("seq")
    n = lax.axis_size("mp")
    _, rows, local_width = queries.shape
    assert GROUP % (local_width // HEAD_DIM // 2) == 0
    depth, out_width = out_weight.shape
    chunk = out_width // n
    width = 256 if chunk % 512 == 0 else HEAD_DIM
    pieces = chunk // 2 // width
    bf16 = jnp.bfloat16
    hbm = pl.BlockSpec(memory_space=pl.ANY)
    total = pl.pallas_call(
        functools.partial(kernel, spans, seqs, n, pieces),
        out_shape=jax.ShapeDtypeStruct((1, rows, chunk), jnp.float32),
        in_specs=[hbm] * 6,
        out_specs=hbm,
        scratch_shapes=[
            pltpu.VMEM((2, rows, local_width // 2), bf16),
            pltpu.VMEM((rows, local_width // 2), bf16),
            pltpu.VMEM((WINDOW, seqs, rows, HEAD_DIM), bf16),
            pltpu.VMEM((WINDOW, seqs, rows, HEAD_DIM), bf16),
            pltpu.VMEM((2, rows, HEAD_DIM), bf16),
            pltpu.VMEM((1, rows), jnp.int32),
            pltpu.SMEM(block_mask.shape, jnp.int32),
            pltpu.VMEM((seqs, 8, rows), jnp.int32),
            pltpu.VMEM((n * pieces, depth, width), bf16),
            pltpu.VMEM((2, 2 * rows, local_width // 2), bf16),
            pltpu.VMEM((n * pieces, 2 * rows, width), jnp.float32),
            pltpu.VMEM((n * pieces, 2 * rows, width), bf16),
            pltpu.VMEM((2, n * pieces, 2 * rows, width), bf16),
            pltpu.VMEM((pieces, 2 * rows, width), jnp.float32),
            pltpu.SemaphoreType.DMA((8,)),
            pltpu.SemaphoreType.DMA((n * pieces,)),
            pltpu.SemaphoreType.DMA((2,)),
            pltpu.SemaphoreType.DMA((WINDOW, seqs, 2)),
            pltpu.SemaphoreType.DMA((WINDOW, seqs, 2)),
            pltpu.SemaphoreType.DMA((seqs,)),
            pltpu.SemaphoreType.DMA((seqs,)),
            pltpu.SemaphoreType.DMA((n * pieces,)),
            pltpu.SemaphoreType.DMA((2, n * pieces)),
            pltpu.SemaphoreType.DMA((pieces,)),
            pltpu.SemaphoreType.DMA((2,)),
            pltpu.SemaphoreType.DMA((2,)),
            pltpu.SemaphoreType.DMA((pieces,)),
            pltpu.SemaphoreType.DMA((pieces,)),
        ],
        compiler_params=pltpu.CompilerParams(
            collective_id=0, has_side_effects=True, vmem_limit_bytes=64 * 1024 * 1024
        ),
    )(queries, keys, values, clip_ids.reshape(1, rows), block_mask, out_weight)
    return total.astype(bf16)


def solution(mesh):
    in_specs = (
        P("span", "seq", "mp"),
        P("span", "seq", None),
        P("span", "seq", None),
        P("seq"),
        P(),
        P("mp", None),
    )
    out_specs = P("span", "seq", "mp")
    return jax.shard_map(
        on_device, mesh=mesh, in_specs=in_specs, out_specs=out_specs, check_vma=False
    )
```

```python
import functools
import math
import jax
import jax.numpy as jnp
from jax import lax
from jax.experimental import pallas as pl
from jax.experimental.pallas import tpu as pltpu
from jax.sharding import PartitionSpec as P

HEAD_DIM = 128
WINDOW = 3
GROUP = 6
MASKED = -1e30
MESH = pl.DeviceIdType.MESH


def kernel(
    spans, seqs, n, pieces,
    q_ref, k_ref, v_ref, clip_ref, mask_ref, w_ref, out_ref,
    qbuf, q_other, kbuf, vbuf, other, own_clip, mask, clips, wbuf, att, ahead, part, sendbuf, recvbuf, outbuf,
    local_sem, w_sem, q_sem, kv_send, kv_recv, clip_send, clip_recv, sum_send, sum_recv, out_sem,
    att_send, att_recv, out_send, out_recv,
):
    _, rows, local_width = q_ref.shape
    head_count = local_width // HEAD_DIM
    width = wbuf.shape[2]
    half = width * pieces
    steps = n * pieces
    c = lax.axis_index("span")
    s = lax.axis_index("seq")
    me = lax.axis_index("mp")
    core = lax.rem(s, 2)
    sibling = {"seq": s + 1 - 2 * core}

    barrier = pltpu.get_barrier_semaphore()
    for j in range(1, WINDOW):
        @pl.when(c >= j)
        def _():
            for s2 in range(seqs):
                pl.semaphore_signal(
                    barrier, inc=1, device_id={"span": c - j, "seq": s2}, device_id_type=MESH
                )
    for d in range(1, seqs):
        pl.semaphore_signal(
            barrier, inc=1, device_id={"seq": lax.rem(s + d, seqs)}, device_id_type=MESH
        )

    @pl.when(me > 0)
    def _():
        pl.semaphore_signal(barrier, inc=1, device_id={"mp": me - 1}, device_id_type=MESH)

    @pl.when(me < n - 1)
    def _():
        pl.semaphore_signal(barrier, inc=1, device_id={"mp": me + 1}, device_id_type=MESH)

    my_heads = head_count // 2
    buddy = s + 1 - 2 * core

    def kv_columns(of):
        group = (me * head_count + of * my_heads) // GROUP
        return pl.ds(pl.multiple_of(group * HEAD_DIM, HEAD_DIM), HEAD_DIM)

    def q_columns(of):
        return pl.ds(pl.multiple_of(of * my_heads * HEAD_DIM, HEAD_DIM), my_heads * HEAD_DIM)

    local = [
        pltpu.make_async_copy(k_ref.at[0, :, kv_columns(core)], kbuf.at[0, s], local_sem.at[0]),
        pltpu.make_async_copy(k_ref.at[0, :, kv_columns(1 - core)], other.at[0], local_sem.at[1]),
        pltpu.make_async_copy(q_ref.at[0, :, q_columns(1 - core)], q_other, local_sem.at[2]),
        pltpu.make_async_copy(v_ref.at[0, :, kv_columns(core)], vbuf.at[0, s], local_sem.at[3]),
        pltpu.make_async_copy(v_ref.at[0, :, kv_columns(1 - core)], other.at[1], local_sem.at[4]),
        pltpu.make_async_copy(clip_ref, own_clip, local_sem.at[5]),
        pltpu.make_async_copy(mask_ref, mask, local_sem.at[6]),
        pltpu.make_async_copy(q_ref.at[0, :, q_columns(core)], qbuf.at[core], local_sem.at[7]),
    ]
    for copy in local:
        copy.start()

    up_count = (n - 1 - me) * pieces
    down_count = me * pieces
    both = jnp.minimum(up_count, down_count)

    def piece_at(i):
        k = jnp.where(i < 2 * both, i // 2, i - both)
        goes_up = jnp.where(i < 2 * both, 1 - lax.rem(i, 2), jnp.where(up_count > down_count, 1, 0))
        moving = jnp.where(goes_up == 1, n - 1 - k // pieces, k // pieces)
        to = jnp.where(i < up_count + down_count, moving, me)
        return to, lax.rem(k, pieces)

    def w_copy(i):
        to, piece = piece_at(i)
        start = (to * 2 + core) * half + piece * width
        return pltpu.make_async_copy(
            w_ref.at[:, pl.ds(pl.multiple_of(start, HEAD_DIM), width)], wbuf.at[i], w_sem.at[i]
        )

    for j in range(1, WINDOW):
        @pl.when(c < j)
        def _():
            kbuf[j] = jnp.zeros(kbuf.shape[1:], kbuf.dtype)
            vbuf[j] = jnp.zeros(vbuf.shape[1:], vbuf.dtype)

    local[5].wait()
    clips[s] = jnp.broadcast_to(own_clip[...], clips.shape[1:])
    for i in range(2):
        local[i].wait()
    later_spans = jnp.minimum(spans - 1 - c, WINDOW - 1)
    z_neighbours = jnp.minimum(me, 1) + jnp.minimum(n - 1 - me, 1)
    pl.semaphore_wait(barrier, seqs - 1 + seqs * later_spans + z_neighbours)

    bufs = (kbuf, vbuf)

    def kv_copy(j, d, a):
        source = bufs[a].at[0, s] if d % 2 == 0 else other.at[a]
        return pltpu.make_async_remote_copy(
            src_ref=source,
            dst_ref=bufs[a].at[j, s],
            send_sem=kv_send.at[j, d, a],
            recv_sem=kv_recv.at[j, s, a],
            device_id={"span": c + j, "seq": lax.rem(s + d, seqs)},
            device_id_type=MESH,
        )

    def arrival(j, s2, a):
        return pltpu.make_async_remote_copy(
            src_ref=bufs[a].at[j, s2],
            dst_ref=bufs[a].at[j, s2],
            send_sem=kv_send.at[0, 0, a],
            recv_sem=kv_recv.at[j, s2, a],
            device_id={"seq": buddy},
            device_id_type=MESH,
        )

    def clip_copy(d, source):
        return pltpu.make_async_remote_copy(
            src_ref=clips.at[source],
            dst_ref=clips.at[source],
            send_sem=clip_send.at[d],
            recv_sem=clip_recv.at[source],
            device_id={"seq": lax.rem(s + d, seqs)},
            device_id_type=MESH,
        )

    def q_copy(at):
        return pltpu.make_async_remote_copy(
            src_ref=q_other,
            dst_ref=qbuf.at[at],
            send_sem=q_sem.at[0],
            recv_sem=q_sem.at[1],
            device_id=sibling,
            device_id_type=MESH,
        )

    for a in range(2):
        for j in range(1, WINDOW):
            @pl.when(c + j < spans)
            def _():
                for d in range(seqs):
                    kv_copy(j, d, a).start()
        for d in range(1, seqs):
            kv_copy(0, d, a).start()
        if a == 0:
            local[2].wait()
            q_copy(core).start()
            for d in range(1, seqs):
                clip_copy(d, s).start()
            local[3].wait()
            local[4].wait()

    def start_w(i, carry):
        w_copy(i).start()
        return carry

    lax.fori_loop(0, steps, start_w, 0)

    def await_block(j, a):
        if j == 0:
            for d in range(1, seqs):
                arrival(0, lax.rem(s + d, seqs), a).wait_recv()
        else:
            @pl.when(c >= j)
            def _():
                for s2 in range(seqs):
                    arrival(j, s2, a).wait_recv()

    for d in range(1, seqs):
        clip_copy(d, lax.rem(s + d, seqs)).wait_recv()
    local[6].wait()

    def clip_square(s2):
        return jnp.broadcast_to(clips[s2, 0:1, :], (rows, rows)).astype(jnp.float32)

    columns = [clip_square(s - core + r).T for r in range(2)]
    same = [[clip_square(s2) == column for s2 in range(seqs)] for column in columns]

    local[7].wait()
    q_copy(1 - core).wait_recv()
    queries = jnp.concatenate(
        [
            qbuf[:, :, i * HEAD_DIM:(i + 1) * HEAD_DIM].reshape(2 * rows, HEAD_DIM)
            for i in range(my_heads)
        ],
        axis=0,
    )
    piece = seqs * rows
    scores = []
    for j in range(WINDOW):
        entry = mask[c, jnp.maximum(c - j, 0)]
        seen = jnp.where((c >= j) & (entry == 1), 0.0, MASKED).astype(jnp.float32)
        bias = jnp.concatenate(
            [
                jnp.concatenate([jnp.where(same[r][s2], seen, MASKED) for s2 in range(seqs)], axis=1)
                for r in range(2)
            ],
            axis=0,
        )
        await_block(j, 0)
        dots = lax.dot_general(
            queries, kbuf[j].reshape(piece, HEAD_DIM), (((1,), (1,)), ((), ())),
            preferred_element_type=jnp.float32,
        )
        scores.append(dots.reshape(my_heads, 2 * rows, piece) + bias[None])
    scores = jnp.concatenate(scores, axis=2)
    top = jnp.max(scores, axis=2, keepdims=True)
    scale = HEAD_DIM ** (-0.5) * math.log2(math.e)
    weights = jnp.exp2((scores - top) * scale).astype(jnp.bfloat16)
    for j in range(WINDOW):
        await_block(j, 1)
    key_count = WINDOW * piece
    values = jnp.concatenate(
        [vbuf[...].reshape(key_count, HEAD_DIM), jnp.ones((key_count, HEAD_DIM), jnp.bfloat16)],
        axis=1,
    )

    att_parts = 2
    att_heads = my_heads // att_parts

    def att_copy(i, source):
        part_columns = pl.ds(i * att_heads * HEAD_DIM, att_heads * HEAD_DIM)
        return pltpu.make_async_remote_copy(
            src_ref=att.at[source, :, part_columns],
            dst_ref=att.at[source, :, part_columns],
            send_sem=att_send.at[i],
            recv_sem=att_recv.at[i],
            device_id=sibling,
            device_id_type=MESH,
        )

    for i in range(att_parts):
        heads = slice(i * att_heads, (i + 1) * att_heads)
        both_sums = jnp.dot(
            weights[heads].reshape(att_heads * 2 * rows, key_count), values,
            preferred_element_type=jnp.float32,
        )
        o = (both_sums[:, :HEAD_DIM] / both_sums[:, HEAD_DIM:]).astype(jnp.bfloat16)
        for h in range(att_heads):
            at = (i * att_heads + h) * HEAD_DIM
            att[core, :, at:at + HEAD_DIM] = o[h * 2 * rows:(h + 1) * 2 * rows]
        att_copy(i, core).start()
    half_depth = my_heads * HEAD_DIM

    def half_product(i, of):
        depth = pl.ds(pl.multiple_of(of * half_depth, half_depth), half_depth)
        return jnp.dot(att[of], wbuf[i, depth, :], preferred_element_type=jnp.float32)

    for i in range(2):
        w_copy(i).wait()
        ahead[i] = half_product(i, core)
    for i in range(att_parts):
        att_copy(i, 1 - core).wait_recv()

    def pass_on(way, at):
        return pltpu.make_async_remote_copy(
            src_ref=sendbuf.at[at],
            dst_ref=recvbuf.at[way, at],
            send_sem=sum_send.at[at],
            recv_sem=sum_recv.at[way, at],
            device_id={"mp": me + 1 - 2 * way},
            device_id_type=MESH,
        )

    def project(i, begun):
        to, piece = piece_at(i)
        at = to * pieces + piece
        if begun:
            product = ahead[i] + half_product(i, 1 - core)
        else:
            w_copy(i).wait()
            product = jnp.dot(
                jnp.concatenate([att[0], att[1]], axis=1), wbuf[i],
                preferred_element_type=jnp.float32,
            )
        part[at] = product

        @pl.when((me == 0) & (to > 0))
        def _():
            sendbuf[at] = product.astype(sendbuf.dtype)
            pass_on(0, at).start()

        @pl.when((me == n - 1) & (to < n - 1))
        def _():
            sendbuf[at] = product.astype(sendbuf.dtype)
            pass_on(1, at).start()

    up_lag = 2 * me - 1
    down_lag = 2 * (n - 1 - me) - 1

    def relay_sums(m):
        up = (n - 1) * pieces - jnp.maximum(m - up_lag, 0) // pieces * pieces + lax.rem(
            jnp.maximum(m - up_lag, 0), pieces
        )

        @pl.when((me > 0) & (m >= up_lag) & (m - up_lag < up_count))
        def _():
            pass_on(0, up).wait_recv()
            sendbuf[up] = (part[up] + recvbuf[0, up].astype(jnp.float32)).astype(sendbuf.dtype)
            pass_on(0, up).start()

        down = jnp.maximum(m - down_lag, 0)

        @pl.when((me < n - 1) & (m >= down_lag) & (m - down_lag < down_count))
        def _():
            pass_on(1, down).wait_recv()
            sendbuf[down] = (part[down] + recvbuf[1, down].astype(jnp.float32)).astype(sendbuf.dtype)
            pass_on(1, down).start()

    def project_and_relay(m, carry):
        project(2 * m, False)
        project(2 * m + 1, False)
        relay_sums(m)
        return carry

    def relay_only(m, carry):
        relay_sums(m)
        return carry

    project(0, True)
    project(1, True)
    relay_sums(0)
    lax.fori_loop(1, steps // 2, project_and_relay, 0)
    last = max((n - 1 - z) * pieces + 2 * z - 1 for z in range(1, n))
    lax.fori_loop(steps // 2, last, relay_only, 0)

    def out_columns(i, of):
        return pl.ds(pl.multiple_of(of * half + i * width, HEAD_DIM), width)

    def out_copy(i):
        return pltpu.make_async_copy(
            outbuf.at[i, pl.ds(pl.multiple_of(core * rows, rows), rows)],
            out_ref.at[0, :, out_columns(i, core)],
            out_sem.at[i],
        )

    def out_to_sibling(i, of):
        return pltpu.make_async_remote_copy(
            src_ref=outbuf.at[i, pl.ds(pl.multiple_of((1 - core) * rows, rows), rows)],
            dst_ref=out_ref.at[0, :, out_columns(i, of)],
            send_sem=out_send.at[i],
            recv_sem=out_recv.at[i],
            device_id=sibling,
            device_id_type=MESH,
        )

    for i in range(pieces):
        at = me * pieces + i

        @pl.when(me > 0)
        def _():
            pass_on(0, at).wait_recv()
            part[at] += recvbuf[0, at].astype(jnp.float32)

        @pl.when(me < n - 1)
        def _():
            pass_on(1, at).wait_recv()
            part[at] += recvbuf[1, at].astype(jnp.float32)

        outbuf[i] = part[at].astype(outbuf.dtype)
        out_to_sibling(i, core).start()
        out_copy(i).start()

    for a in range(2):
        for j in range(1, WINDOW):
            @pl.when(c + j < spans)
            def _():
                for d in range(seqs):
                    kv_copy(j, d, a).wait_send()
        for d in range(1, seqs):
            kv_copy(0, d, a).wait_send()
    q_copy(core).wait_send()
    for d in range(1, seqs):
        clip_copy(d, s).wait_send()

    def sent(i, carry):
        @pl.when(i // pieces != me)
        def _():
            pass_on(0, i).wait_send()

        return carry

    lax.fori_loop(0, steps, sent, 0)
    for i in range(att_parts):
        att_copy(i, core).wait_send()
    for i in range(pieces):
        out_copy(i).wait()
        out_to_sibling(i, core).wait_send()
        out_to_sibling(i, 1 - core).wait_recv()


def hand_over(x_ref, y_ref, sems):
    bands = sems.shape[0]
    height = x_ref.shape[1] // bands
    copies = [
        pltpu.make_async_copy(
            x_ref.at[0, pl.ds(i * height, height)], y_ref.at[0, pl.ds(i * height, height)], sems.at[i]
        )
        for i in range(bands)
    ]
    for copy in copies:
        copy.start()
    for copy in copies:
        copy.wait()


def on_device(queries, keys, values, clip_ids, block_mask, out_weight):
    spans = lax.axis_size("span")
    seqs = lax.axis_size("seq")
    n = lax.axis_size("mp")
    _, rows, local_width = queries.shape
    assert GROUP % (local_width // HEAD_DIM // 2) == 0
    depth, out_width = out_weight.shape
    chunk = out_width // n
    width = 256 if chunk % 512 == 0 else HEAD_DIM
    pieces = chunk // 2 // width
    bf16 = jnp.bfloat16
    hbm = pl.BlockSpec(memory_space=pl.ANY)
    total = pl.pallas_call(
        functools.partial(kernel, spans, seqs, n, pieces),
        out_shape=jax.ShapeDtypeStruct((1, rows, chunk), bf16),
        in_specs=[hbm] * 6,
        out_specs=hbm,
        scratch_shapes=[
            pltpu.VMEM((2, rows, local_width // 2), bf16),
            pltpu.VMEM((rows, local_width // 2), bf16),
            pltpu.VMEM((WINDOW, seqs, rows, HEAD_DIM), bf16),
            pltpu.VMEM((WINDOW, seqs, rows, HEAD_DIM), bf16),
            pltpu.VMEM((2, rows, HEAD_DIM), bf16),
            pltpu.VMEM((1, rows), jnp.int32),
            pltpu.SMEM(block_mask.shape, jnp.int32),
            pltpu.VMEM((seqs, 8, rows), jnp.int32),
            pltpu.VMEM((n * pieces, depth, width), bf16),
            pltpu.VMEM((2, 2 * rows, local_width // 2), bf16),
            pltpu.VMEM((2, 2 * rows, width), jnp.float32),
            pltpu.VMEM((n * pieces, 2 * rows, width), jnp.float32),
            pltpu.VMEM((n * pieces, 2 * rows, width), bf16),
            pltpu.VMEM((2, n * pieces, 2 * rows, width), bf16),
            pltpu.VMEM((pieces, 2 * rows, width), bf16),
            pltpu.SemaphoreType.DMA((8,)),
            pltpu.SemaphoreType.DMA((n * pieces,)),
            pltpu.SemaphoreType.DMA((2,)),
            pltpu.SemaphoreType.DMA((WINDOW, seqs, 2)),
            pltpu.SemaphoreType.DMA((WINDOW, seqs, 2)),
            pltpu.SemaphoreType.DMA((seqs,)),
            pltpu.SemaphoreType.DMA((seqs,)),
            pltpu.SemaphoreType.DMA((n * pieces,)),
            pltpu.SemaphoreType.DMA((2, n * pieces)),
            pltpu.SemaphoreType.DMA((pieces,)),
            pltpu.SemaphoreType.DMA((2,)),
            pltpu.SemaphoreType.DMA((2,)),
            pltpu.SemaphoreType.DMA((pieces,)),
            pltpu.SemaphoreType.DMA((pieces,)),
        ],
        compiler_params=pltpu.CompilerParams(
            collective_id=0, has_side_effects=True, vmem_limit_bytes=64 * 1024 * 1024
        ),
    )(queries, keys, values, clip_ids.reshape(1, rows), block_mask, out_weight)
    bands = rows // 16
    return pl.pallas_call(
        hand_over,
        out_shape=jax.ShapeDtypeStruct(total.shape, bf16),
        in_specs=[hbm],
        out_specs=hbm,
        scratch_shapes=[pltpu.SemaphoreType.DMA((bands,))],
    )(total)


def solution(mesh):
    in_specs = (
        P("span", "seq", "mp"),
        P("span", "seq", None),
        P("span", "seq", None),
        P("seq"),
        P(),
        P("mp", None),
    )
    out_specs = P("span", "seq", "mp")
    return jax.shard_map(
        on_device, mesh=mesh, in_specs=in_specs, out_specs=out_specs, check_vma=False
    )
```

```python
import functools
import math
import jax
import jax.numpy as jnp
from jax import lax
from jax.experimental import pallas as pl
from jax.experimental.pallas import tpu as pltpu
from jax.sharding import PartitionSpec as P

HEAD_DIM = 128
WINDOW = 3
GROUP = 6
MASKED = -1e30
MESH = pl.DeviceIdType.MESH


def kernel(
    spans, seqs, n, pieces,
    q_ref, k_ref, v_ref, clip_ref, mask_ref, w_ref, out_ref,
    qbuf, q_other, kbuf, vbuf, other, own_clip, mask, clips, wbuf, att, part, sendbuf, recvbuf, outbuf,
    local_sem, w_sem, q_sem, kv_send, kv_recv, clip_send, clip_recv, sum_send, sum_recv, out_sem,
    att_send, att_recv, out_send, out_recv,
):
    _, rows, local_width = q_ref.shape
    head_count = local_width // HEAD_DIM
    width = wbuf.shape[2]
    half = width * pieces
    steps = n * pieces
    c = lax.axis_index("span")
    s = lax.axis_index("seq")
    me = lax.axis_index("mp")
    core = lax.rem(s, 2)
    sibling = {"seq": s + 1 - 2 * core}

    barrier = pltpu.get_barrier_semaphore()
    for j in range(1, WINDOW):
        @pl.when(c >= j)
        def _():
            for s2 in range(seqs):
                pl.semaphore_signal(
                    barrier, inc=1, device_id={"span": c - j, "seq": s2}, device_id_type=MESH
                )
    for d in range(1, seqs):
        pl.semaphore_signal(
            barrier, inc=1, device_id={"seq": lax.rem(s + d, seqs)}, device_id_type=MESH
        )

    @pl.when(me > 0)
    def _():
        pl.semaphore_signal(barrier, inc=1, device_id={"mp": me - 1}, device_id_type=MESH)

    @pl.when(me < n - 1)
    def _():
        pl.semaphore_signal(barrier, inc=1, device_id={"mp": me + 1}, device_id_type=MESH)

    my_heads = head_count // 2
    buddy = s + 1 - 2 * core

    def kv_columns(of):
        group = (me * head_count + of * my_heads) // GROUP
        return pl.ds(pl.multiple_of(group * HEAD_DIM, HEAD_DIM), HEAD_DIM)

    def q_columns(of):
        return pl.ds(pl.multiple_of(of * my_heads * HEAD_DIM, HEAD_DIM), my_heads * HEAD_DIM)

    local = [
        pltpu.make_async_copy(k_ref.at[0, :, kv_columns(core)], kbuf.at[0, s], local_sem.at[0]),
        pltpu.make_async_copy(k_ref.at[0, :, kv_columns(1 - core)], other.at[0], local_sem.at[1]),
        pltpu.make_async_copy(q_ref.at[0, :, q_columns(1 - core)], q_other, local_sem.at[2]),
        pltpu.make_async_copy(v_ref.at[0, :, kv_columns(core)], vbuf.at[0, s], local_sem.at[3]),
        pltpu.make_async_copy(v_ref.at[0, :, kv_columns(1 - core)], other.at[1], local_sem.at[4]),
        pltpu.make_async_copy(clip_ref, own_clip, local_sem.at[5]),
        pltpu.make_async_copy(mask_ref, mask, local_sem.at[6]),
        pltpu.make_async_copy(q_ref.at[0, :, q_columns(core)], qbuf.at[core], local_sem.at[7]),
    ]
    for copy in local:
        copy.start()

    up_count = (n - 1 - me) * pieces
    down_count = me * pieces
    both = jnp.minimum(up_count, down_count)

    def piece_at(i):
        k = jnp.where(i < 2 * both, i // 2, i - both)
        goes_up = jnp.where(i < 2 * both, 1 - lax.rem(i, 2), jnp.where(up_count > down_count, 1, 0))
        moving = jnp.where(goes_up == 1, n - 1 - k // pieces, k // pieces)
        to = jnp.where(i < up_count + down_count, moving, me)
        return to, lax.rem(k, pieces)

    def w_copy(i):
        to, piece = piece_at(i)
        start = (to * 2 + core) * half + piece * width
        return pltpu.make_async_copy(
            w_ref.at[:, pl.ds(pl.multiple_of(start, HEAD_DIM), width)], wbuf.at[i], w_sem.at[i]
        )

    for j in range(1, WINDOW):
        @pl.when(c < j)
        def _():
            kbuf[j] = jnp.zeros(kbuf.shape[1:], kbuf.dtype)
            vbuf[j] = jnp.zeros(vbuf.shape[1:], vbuf.dtype)

    local[5].wait()
    clips[s] = jnp.broadcast_to(own_clip[...], clips.shape[1:])
    for i in range(2):
        local[i].wait()
    later_spans = jnp.minimum(spans - 1 - c, WINDOW - 1)
    z_neighbours = jnp.minimum(me, 1) + jnp.minimum(n - 1 - me, 1)
    pl.semaphore_wait(barrier, seqs - 1 + seqs * later_spans + z_neighbours)

    bufs = (kbuf, vbuf)

    def kv_copy(j, d, a):
        source = bufs[a].at[0, s] if d % 2 == 0 else other.at[a]
        return pltpu.make_async_remote_copy(
            src_ref=source,
            dst_ref=bufs[a].at[j, s],
            send_sem=kv_send.at[j, d, a],
            recv_sem=kv_recv.at[j, s, a],
            device_id={"span": c + j, "seq": lax.rem(s + d, seqs)},
            device_id_type=MESH,
        )

    def arrival(j, s2, a):
        return pltpu.make_async_remote_copy(
            src_ref=bufs[a].at[j, s2],
            dst_ref=bufs[a].at[j, s2],
            send_sem=kv_send.at[0, 0, a],
            recv_sem=kv_recv.at[j, s2, a],
            device_id={"seq": buddy},
            device_id_type=MESH,
        )

    def clip_copy(d, source):
        return pltpu.make_async_remote_copy(
            src_ref=clips.at[source],
            dst_ref=clips.at[source],
            send_sem=clip_send.at[d],
            recv_sem=clip_recv.at[source],
            device_id={"seq": lax.rem(s + d, seqs)},
            device_id_type=MESH,
        )

    def q_copy(at):
        return pltpu.make_async_remote_copy(
            src_ref=q_other,
            dst_ref=qbuf.at[at],
            send_sem=q_sem.at[0],
            recv_sem=q_sem.at[1],
            device_id=sibling,
            device_id_type=MESH,
        )

    for a in range(2):
        for j in range(1, WINDOW):
            @pl.when(c + j < spans)
            def _():
                for d in range(seqs):
                    kv_copy(j, d, a).start()
        for d in range(1, seqs):
            kv_copy(0, d, a).start()
        if a == 0:
            local[2].wait()
            q_copy(core).start()
            for d in range(1, seqs):
                clip_copy(d, s).start()
            local[3].wait()
            local[4].wait()

    def start_w(i, carry):
        w_copy(i).start()
        return carry

    lax.fori_loop(0, steps, start_w, 0)

    def await_block(j, a):
        if j == 0:
            for d in range(1, seqs):
                arrival(0, lax.rem(s + d, seqs), a).wait_recv()
        else:
            @pl.when(c >= j)
            def _():
                for s2 in range(seqs):
                    arrival(j, s2, a).wait_recv()

    for d in range(1, seqs):
        clip_copy(d, lax.rem(s + d, seqs)).wait_recv()
    local[6].wait()

    def clip_square(s2):
        return jnp.broadcast_to(clips[s2, 0:1, :], (rows, rows)).astype(jnp.float32)

    columns = [clip_square(s - core + r).T for r in range(2)]
    same = [[clip_square(s2) == column for s2 in range(seqs)] for column in columns]

    local[7].wait()
    q_copy(1 - core).wait_recv()
    queries = jnp.concatenate(
        [
            qbuf[:, :, i * HEAD_DIM:(i + 1) * HEAD_DIM].reshape(2 * rows, HEAD_DIM)
            for i in range(my_heads)
        ],
        axis=0,
    )
    piece = seqs * rows
    scores = []
    for j in range(WINDOW):
        entry = mask[c, jnp.maximum(c - j, 0)]
        seen = jnp.where((c >= j) & (entry == 1), 0.0, MASKED).astype(jnp.float32)
        bias = jnp.concatenate(
            [
                jnp.concatenate([jnp.where(same[r][s2], seen, MASKED) for s2 in range(seqs)], axis=1)
                for r in range(2)
            ],
            axis=0,
        )
        await_block(j, 0)
        dots = lax.dot_general(
            queries, kbuf[j].reshape(piece, HEAD_DIM), (((1,), (1,)), ((), ())),
            preferred_element_type=jnp.float32,
        )
        scores.append(dots.reshape(my_heads, 2 * rows, piece) + bias[None])
    scores = jnp.concatenate(scores, axis=2)
    top = jnp.max(scores, axis=2, keepdims=True)
    scale = HEAD_DIM ** (-0.5) * math.log2(math.e)
    weights = jnp.exp2((scores - top) * scale).astype(jnp.bfloat16)
    for j in range(WINDOW):
        await_block(j, 1)
    key_count = WINDOW * piece
    values = jnp.concatenate(
        [vbuf[...].reshape(key_count, HEAD_DIM), jnp.ones((key_count, HEAD_DIM), jnp.bfloat16)],
        axis=1,
    )

    att_parts = 2
    att_heads = my_heads // att_parts

    def att_copy(i, source):
        part_columns = pl.ds(i * att_heads * HEAD_DIM, att_heads * HEAD_DIM)
        return pltpu.make_async_remote_copy(
            src_ref=att.at[source, :, part_columns],
            dst_ref=att.at[source, :, part_columns],
            send_sem=att_send.at[i],
            recv_sem=att_recv.at[i],
            device_id=sibling,
            device_id_type=MESH,
        )

    for i in range(att_parts):
        heads = slice(i * att_heads, (i + 1) * att_heads)
        both_sums = jnp.dot(
            weights[heads].reshape(att_heads * 2 * rows, key_count), values,
            preferred_element_type=jnp.float32,
        )
        o = (both_sums[:, :HEAD_DIM] / both_sums[:, HEAD_DIM:]).astype(jnp.bfloat16)
        for h in range(att_heads):
            at = (i * att_heads + h) * HEAD_DIM
            att[core, :, at:at + HEAD_DIM] = o[h * 2 * rows:(h + 1) * 2 * rows]
        att_copy(i, core).start()
    for i in range(att_parts):
        att_copy(i, 1 - core).wait_recv()

    def pass_on(way, at):
        return pltpu.make_async_remote_copy(
            src_ref=sendbuf.at[at],
            dst_ref=recvbuf.at[way, at],
            send_sem=sum_send.at[at],
            recv_sem=sum_recv.at[way, at],
            device_id={"mp": me + 1 - 2 * way},
            device_id_type=MESH,
        )

    def project(i):
        to, piece = piece_at(i)
        at = to * pieces + piece
        w_copy(i).wait()
        product = jnp.dot(
            jnp.concatenate([att[0], att[1]], axis=1), wbuf[i], preferred_element_type=jnp.float32
        )
        part[at] = product

        @pl.when((me == 0) & (to > 0))
        def _():
            sendbuf[at] = product.astype(sendbuf.dtype)
            pass_on(0, at).start()

        @pl.when((me == n - 1) & (to < n - 1))
        def _():
            sendbuf[at] = product.astype(sendbuf.dtype)
            pass_on(1, at).start()

    up_lag = 2 * me - 1
    down_lag = 2 * (n - 1 - me) - 1

    def relay_sums(m):
        up = (n - 1) * pieces - jnp.maximum(m - up_lag, 0) // pieces * pieces + lax.rem(
            jnp.maximum(m - up_lag, 0), pieces
        )

        @pl.when((me > 0) & (m >= up_lag) & (m - up_lag < up_count))
        def _():
            pass_on(0, up).wait_recv()
            sendbuf[up] = (part[up] + recvbuf[0, up].astype(jnp.float32)).astype(sendbuf.dtype)
            pass_on(0, up).start()

        down = jnp.maximum(m - down_lag, 0)

        @pl.when((me < n - 1) & (m >= down_lag) & (m - down_lag < down_count))
        def _():
            pass_on(1, down).wait_recv()
            sendbuf[down] = (part[down] + recvbuf[1, down].astype(jnp.float32)).astype(sendbuf.dtype)
            pass_on(1, down).start()

    def project_and_relay(m, carry):
        project(2 * m)
        project(2 * m + 1)
        relay_sums(m)
        return carry

    def relay_only(m, carry):
        relay_sums(m)
        return carry

    lax.fori_loop(0, steps // 2, project_and_relay, 0)
    last = max((n - 1 - z) * pieces + 2 * z - 1 for z in range(1, n))
    lax.fori_loop(steps // 2, last, relay_only, 0)

    def out_columns(i, of):
        return pl.ds(pl.multiple_of(of * half + i * width, HEAD_DIM), width)

    def out_copy(i):
        return pltpu.make_async_copy(
            outbuf.at[i, pl.ds(pl.multiple_of(core * rows, rows), rows)],
            out_ref.at[0, :, out_columns(i, core)],
            out_sem.at[i],
        )

    def out_to_sibling(i, of):
        return pltpu.make_async_remote_copy(
            src_ref=outbuf.at[i, pl.ds(pl.multiple_of((1 - core) * rows, rows), rows)],
            dst_ref=out_ref.at[0, :, out_columns(i, of)],
            send_sem=out_send.at[i],
            recv_sem=out_recv.at[i],
            device_id=sibling,
            device_id_type=MESH,
        )

    for i in range(pieces):
        at = me * pieces + i

        @pl.when(me > 0)
        def _():
            pass_on(0, at).wait_recv()
            part[at] += recvbuf[0, at].astype(jnp.float32)

        @pl.when(me < n - 1)
        def _():
            pass_on(1, at).wait_recv()
            part[at] += recvbuf[1, at].astype(jnp.float32)

        outbuf[i] = part[at].astype(outbuf.dtype)
        out_to_sibling(i, core).start()
        out_copy(i).start()

    for a in range(2):
        for j in range(1, WINDOW):
            @pl.when(c + j < spans)
            def _():
                for d in range(seqs):
                    kv_copy(j, d, a).wait_send()
        for d in range(1, seqs):
            kv_copy(0, d, a).wait_send()
    q_copy(core).wait_send()
    for d in range(1, seqs):
        clip_copy(d, s).wait_send()

    def sent(i, carry):
        @pl.when(i // pieces != me)
        def _():
            pass_on(0, i).wait_send()

        return carry

    lax.fori_loop(0, steps, sent, 0)
    for i in range(att_parts):
        att_copy(i, core).wait_send()
    for i in range(pieces):
        out_copy(i).wait()
        out_to_sibling(i, core).wait_send()
        out_to_sibling(i, 1 - core).wait_recv()


def on_device(queries, keys, values, clip_ids, block_mask, out_weight):
    spans = lax.axis_size("span")
    seqs = lax.axis_size("seq")
    n = lax.axis_size("mp")
    _, rows, local_width = queries.shape
    assert GROUP % (local_width // HEAD_DIM // 2) == 0
    depth, out_width = out_weight.shape
    chunk = out_width // n
    width = 256 if chunk % 512 == 0 else HEAD_DIM
    pieces = chunk // 2 // width
    bf16 = jnp.bfloat16
    hbm = pl.BlockSpec(memory_space=pl.ANY)
    return pl.pallas_call(
        functools.partial(kernel, spans, seqs, n, pieces),
        out_shape=jax.ShapeDtypeStruct((1, rows, chunk), bf16),
        in_specs=[hbm] * 6,
        out_specs=hbm,
        scratch_shapes=[
            pltpu.VMEM((2, rows, local_width // 2), bf16),
            pltpu.VMEM((rows, local_width // 2), bf16),
            pltpu.VMEM((WINDOW, seqs, rows, HEAD_DIM), bf16),
            pltpu.VMEM((WINDOW, seqs, rows, HEAD_DIM), bf16),
            pltpu.VMEM((2, rows, HEAD_DIM), bf16),
            pltpu.VMEM((1, rows), jnp.int32),
            pltpu.SMEM(block_mask.shape, jnp.int32),
            pltpu.VMEM((seqs, 8, rows), jnp.int32),
            pltpu.VMEM((n * pieces, depth, width), bf16),
            pltpu.VMEM((2, 2 * rows, local_width // 2), bf16),
            pltpu.VMEM((n * pieces, 2 * rows, width), jnp.float32),
            pltpu.VMEM((n * pieces, 2 * rows, width), bf16),
            pltpu.VMEM((2, n * pieces, 2 * rows, width), bf16),
            pltpu.VMEM((pieces, 2 * rows, width), bf16),
            pltpu.SemaphoreType.DMA((8,)),
            pltpu.SemaphoreType.DMA((n * pieces,)),
            pltpu.SemaphoreType.DMA((2,)),
            pltpu.SemaphoreType.DMA((WINDOW, seqs, 2)),
            pltpu.SemaphoreType.DMA((WINDOW, seqs, 2)),
            pltpu.SemaphoreType.DMA((seqs,)),
            pltpu.SemaphoreType.DMA((seqs,)),
            pltpu.SemaphoreType.DMA((n * pieces,)),
            pltpu.SemaphoreType.DMA((2, n * pieces)),
            pltpu.SemaphoreType.DMA((pieces,)),
            pltpu.SemaphoreType.DMA((2,)),
            pltpu.SemaphoreType.DMA((2,)),
            pltpu.SemaphoreType.DMA((pieces,)),
            pltpu.SemaphoreType.DMA((pieces,)),
        ],
        compiler_params=pltpu.CompilerParams(
            collective_id=0, has_side_effects=True, vmem_limit_bytes=64 * 1024 * 1024
        ),
    )(queries, keys, values, clip_ids.reshape(1, rows), block_mask, out_weight)


def solution(mesh):
    in_specs = (
        P("span", "seq", "mp"),
        P("span", "seq", None),
        P("span", "seq", None),
        P("seq"),
        P(),
        P("mp", None),
    )
    out_specs = P("span", "seq", "mp")
    return jax.shard_map(
        on_device, mesh=mesh, in_specs=in_specs, out_specs=out_specs, check_vma=False
    )
```

```python
import functools
import math
import jax
import jax.numpy as jnp
from jax import lax
from jax.experimental import pallas as pl
from jax.experimental.pallas import tpu as pltpu
from jax.sharding import PartitionSpec as P

HEAD_DIM = 128
WINDOW = 3
GROUP = 6
MASKED = -1e30
MESH = pl.DeviceIdType.MESH


def kernel(
    spans, seqs, n, pieces,
    q_ref, k_ref, v_ref, clip_ref, mask_ref, w_ref, out_ref,
    qbuf, q_other, kbuf, vbuf, other, own_clip, mask, clips, wbuf, att, part, sendbuf, recvbuf, outbuf,
    local_sem, w_sem, q_sem, kv_send, kv_recv, clip_send, clip_recv, sum_send, sum_recv, out_sem,
    att_send, att_recv, out_send, out_recv,
):
    _, rows, local_width = q_ref.shape
    head_count = local_width // HEAD_DIM
    width = wbuf.shape[2]
    half = width * pieces
    steps = n * pieces
    c = lax.axis_index("span")
    s = lax.axis_index("seq")
    me = lax.axis_index("mp")
    core = lax.rem(s, 2)
    sibling = {"seq": s + 1 - 2 * core}

    barrier = pltpu.get_barrier_semaphore()
    for j in range(1, WINDOW):
        @pl.when(c >= j)
        def _():
            for s2 in range(seqs):
                pl.semaphore_signal(
                    barrier, inc=1, device_id={"span": c - j, "seq": s2}, device_id_type=MESH
                )
    for d in range(1, seqs):
        pl.semaphore_signal(
            barrier, inc=1, device_id={"seq": lax.rem(s + d, seqs)}, device_id_type=MESH
        )

    @pl.when(me > 0)
    def _():
        pl.semaphore_signal(barrier, inc=1, device_id={"mp": me - 1}, device_id_type=MESH)

    @pl.when(me < n - 1)
    def _():
        pl.semaphore_signal(barrier, inc=1, device_id={"mp": me + 1}, device_id_type=MESH)

    my_heads = head_count // 2
    buddy = s + 1 - 2 * core

    def kv_columns(of):
        group = (me * head_count + of * my_heads) // GROUP
        return pl.ds(pl.multiple_of(group * HEAD_DIM, HEAD_DIM), HEAD_DIM)

    def q_columns(of):
        return pl.ds(pl.multiple_of(of * my_heads * HEAD_DIM, HEAD_DIM), my_heads * HEAD_DIM)

    local = [
        pltpu.make_async_copy(k_ref.at[0, :, kv_columns(core)], kbuf.at[0, s], local_sem.at[0]),
        pltpu.make_async_copy(k_ref.at[0, :, kv_columns(1 - core)], other.at[0], local_sem.at[1]),
        pltpu.make_async_copy(q_ref.at[0, :, q_columns(1 - core)], q_other, local_sem.at[2]),
        pltpu.make_async_copy(v_ref.at[0, :, kv_columns(core)], vbuf.at[0, s], local_sem.at[3]),
        pltpu.make_async_copy(v_ref.at[0, :, kv_columns(1 - core)], other.at[1], local_sem.at[4]),
        pltpu.make_async_copy(clip_ref, own_clip, local_sem.at[5]),
        pltpu.make_async_copy(mask_ref, mask, local_sem.at[6]),
        pltpu.make_async_copy(q_ref.at[0, :, q_columns(core)], qbuf.at[core], local_sem.at[7]),
    ]
    for copy in local:
        copy.start()

    up_count = (n - 1 - me) * pieces
    down_count = me * pieces
    both = jnp.minimum(up_count, down_count)

    def piece_at(i):
        k = jnp.where(i < 2 * both, i // 2, i - both)
        goes_up = jnp.where(i < 2 * both, 1 - lax.rem(i, 2), jnp.where(up_count > down_count, 1, 0))
        moving = jnp.where(goes_up == 1, n - 1 - k // pieces, k // pieces)
        to = jnp.where(i < up_count + down_count, moving, me)
        return to, lax.rem(k, pieces)

    def w_copy(i):
        to, piece = piece_at(i)
        start = (to * 2 + core) * half + piece * width
        return pltpu.make_async_copy(
            w_ref.at[:, pl.ds(pl.multiple_of(start, HEAD_DIM), width)], wbuf.at[i], w_sem.at[i]
        )

    for j in range(1, WINDOW):
        @pl.when(c < j)
        def _():
            kbuf[j] = jnp.zeros(kbuf.shape[1:], kbuf.dtype)
            vbuf[j] = jnp.zeros(vbuf.shape[1:], vbuf.dtype)

    local[5].wait()
    clips[s] = jnp.broadcast_to(own_clip[...], clips.shape[1:])
    for i in range(2):
        local[i].wait()
    later_spans = jnp.minimum(spans - 1 - c, WINDOW - 1)
    z_neighbours = jnp.minimum(me, 1) + jnp.minimum(n - 1 - me, 1)
    pl.semaphore_wait(barrier, seqs - 1 + seqs * later_spans + z_neighbours)

    bufs = (kbuf, vbuf)

    def kv_copy(j, d, a):
        source = bufs[a].at[0, s] if d % 2 == 0 else other.at[a]
        return pltpu.make_async_remote_copy(
            src_ref=source,
            dst_ref=bufs[a].at[j, s],
            send_sem=kv_send.at[j, d, a],
            recv_sem=kv_recv.at[j, s, a],
            device_id={"span": c + j, "seq": lax.rem(s + d, seqs)},
            device_id_type=MESH,
        )

    def arrival(j, s2, a):
        return pltpu.make_async_remote_copy(
            src_ref=bufs[a].at[j, s2],
            dst_ref=bufs[a].at[j, s2],
            send_sem=kv_send.at[0, 0, a],
            recv_sem=kv_recv.at[j, s2, a],
            device_id={"seq": buddy},
            device_id_type=MESH,
        )

    def clip_copy(d, source):
        return pltpu.make_async_remote_copy(
            src_ref=clips.at[source],
            dst_ref=clips.at[source],
            send_sem=clip_send.at[d],
            recv_sem=clip_recv.at[source],
            device_id={"seq": lax.rem(s + d, seqs)},
            device_id_type=MESH,
        )

    def q_copy(at):
        return pltpu.make_async_remote_copy(
            src_ref=q_other,
            dst_ref=qbuf.at[at],
            send_sem=q_sem.at[0],
            recv_sem=q_sem.at[1],
            device_id=sibling,
            device_id_type=MESH,
        )

    for a in range(2):
        for j in range(1, WINDOW):
            @pl.when(c + j < spans)
            def _():
                for d in range(seqs):
                    kv_copy(j, d, a).start()
        for d in range(1, seqs):
            kv_copy(0, d, a).start()
        if a == 0:
            local[2].wait()
            q_copy(core).start()
            for d in range(1, seqs):
                clip_copy(d, s).start()
            local[3].wait()
            local[4].wait()

    def start_w(i, carry):
        w_copy(i).start()
        return carry

    lax.fori_loop(0, steps, start_w, 0)

    def await_block(j, a):
        if j == 0:
            for d in range(1, seqs):
                arrival(0, lax.rem(s + d, seqs), a).wait_recv()
        else:
            @pl.when(c >= j)
            def _():
                for s2 in range(seqs):
                    arrival(j, s2, a).wait_recv()

    for d in range(1, seqs):
        clip_copy(d, lax.rem(s + d, seqs)).wait_recv()
    local[6].wait()

    def clip_square(s2):
        return jnp.broadcast_to(clips[s2, 0:1, :], (rows, rows)).astype(jnp.float32)

    columns = [clip_square(s - core + r).T for r in range(2)]
    same = [[clip_square(s2) == column for s2 in range(seqs)] for column in columns]

    local[7].wait()
    q_copy(1 - core).wait_recv()
    queries = jnp.concatenate(
        [
            qbuf[:, :, i * HEAD_DIM:(i + 1) * HEAD_DIM].reshape(2 * rows, HEAD_DIM)
            for i in range(my_heads)
        ],
        axis=0,
    )
    piece = seqs * rows
    scores = []
    for j in range(WINDOW):
        entry = mask[c, jnp.maximum(c - j, 0)]
        seen = jnp.where((c >= j) & (entry == 1), 0.0, MASKED).astype(jnp.float32)
        bias = jnp.concatenate(
            [
                jnp.concatenate([jnp.where(same[r][s2], seen, MASKED) for s2 in range(seqs)], axis=1)
                for r in range(2)
            ],
            axis=0,
        )
        await_block(j, 0)
        dots = lax.dot_general(
            queries, kbuf[j].reshape(piece, HEAD_DIM), (((1,), (1,)), ((), ())),
            preferred_element_type=jnp.float32,
        )
        scores.append(dots.reshape(my_heads, 2 * rows, piece) + bias[None])
    scores = jnp.concatenate(scores, axis=2)
    top = jnp.max(scores, axis=2, keepdims=True)
    scale = HEAD_DIM ** (-0.5) * math.log2(math.e)
    weights = jnp.exp2((scores - top) * scale).astype(jnp.bfloat16)
    for j in range(WINDOW):
        await_block(j, 1)
    key_count = WINDOW * piece
    values = jnp.concatenate(
        [vbuf[...].reshape(key_count, HEAD_DIM), jnp.ones((key_count, HEAD_DIM), jnp.bfloat16)],
        axis=1,
    )

    att_parts = 2
    att_heads = my_heads // att_parts

    def att_copy(i, source):
        part_columns = pl.ds(i * att_heads * HEAD_DIM, att_heads * HEAD_DIM)
        return pltpu.make_async_remote_copy(
            src_ref=att.at[source, :, part_columns],
            dst_ref=att.at[source, :, part_columns],
            send_sem=att_send.at[i],
            recv_sem=att_recv.at[i],
            device_id=sibling,
            device_id_type=MESH,
        )

    for i in range(att_parts):
        heads = slice(i * att_heads, (i + 1) * att_heads)
        both_sums = jnp.dot(
            weights[heads].reshape(att_heads * 2 * rows, key_count), values,
            preferred_element_type=jnp.float32,
        )
        o = (both_sums[:, :HEAD_DIM] / both_sums[:, HEAD_DIM:]).astype(jnp.bfloat16)
        for h in range(att_heads):
            at = (i * att_heads + h) * HEAD_DIM
            att[core, :, at:at + HEAD_DIM] = o[h * 2 * rows:(h + 1) * 2 * rows]
        att_copy(i, core).start()
    for i in range(att_parts):
        att_copy(i, 1 - core).wait_recv()

    def pass_on(way, at):
        return pltpu.make_async_remote_copy(
            src_ref=sendbuf.at[at],
            dst_ref=recvbuf.at[way, at],
            send_sem=sum_send.at[at],
            recv_sem=sum_recv.at[way, at],
            device_id={"mp": me + 1 - 2 * way},
            device_id_type=MESH,
        )

    def project(i):
        to, piece = piece_at(i)
        at = to * pieces + piece
        w_copy(i).wait()
        product = jnp.dot(
            jnp.concatenate([att[0], att[1]], axis=1), wbuf[i], preferred_element_type=jnp.float32
        )
        part[at] = product

        @pl.when((me == 0) & (to > 0))
        def _():
            sendbuf[at] = product.astype(sendbuf.dtype)
            pass_on(0, at).start()

        @pl.when((me == n - 1) & (to < n - 1))
        def _():
            sendbuf[at] = product.astype(sendbuf.dtype)
            pass_on(1, at).start()

    up_lag = 2 * me - 1
    down_lag = 2 * (n - 1 - me) - 1

    def relay_sums(m):
        up = (n - 1) * pieces - jnp.maximum(m - up_lag, 0) // pieces * pieces + lax.rem(
            jnp.maximum(m - up_lag, 0), pieces
        )

        @pl.when((me > 0) & (m >= up_lag) & (m - up_lag < up_count))
        def _():
            pass_on(0, up).wait_recv()
            sendbuf[up] = (part[up] + recvbuf[0, up].astype(jnp.float32)).astype(sendbuf.dtype)
            pass_on(0, up).start()

        down = jnp.maximum(m - down_lag, 0)

        @pl.when((me < n - 1) & (m >= down_lag) & (m - down_lag < down_count))
        def _():
            pass_on(1, down).wait_recv()
            sendbuf[down] = (part[down] + recvbuf[1, down].astype(jnp.float32)).astype(sendbuf.dtype)
            pass_on(1, down).start()

    def project_and_relay(m, carry):
        project(2 * m)
        project(2 * m + 1)
        relay_sums(m)
        return carry

    def relay_only(m, carry):
        relay_sums(m)
        return carry

    lax.fori_loop(0, steps // 2, project_and_relay, 0)
    last = max((n - 1 - z) * pieces + 2 * z - 1 for z in range(1, n))
    lax.fori_loop(steps // 2, last, relay_only, 0)

    def out_columns(i, of):
        return pl.ds(pl.multiple_of(of * half + i * width, HEAD_DIM), width)

    def out_copy(i):
        return pltpu.make_async_copy(
            outbuf.at[i, pl.ds(pl.multiple_of(core * rows, rows), rows)],
            out_ref.at[0, :, out_columns(i, core)],
            out_sem.at[i],
        )

    def out_to_sibling(i, of):
        return pltpu.make_async_remote_copy(
            src_ref=outbuf.at[i, pl.ds(pl.multiple_of((1 - core) * rows, rows), rows)],
            dst_ref=out_ref.at[0, :, out_columns(i, of)],
            send_sem=out_send.at[i],
            recv_sem=out_recv.at[i],
            device_id=sibling,
            device_id_type=MESH,
        )

    for i in range(pieces):
        at = me * pieces + i

        @pl.when(me > 0)
        def _():
            pass_on(0, at).wait_recv()
            part[at] += recvbuf[0, at].astype(jnp.float32)

        @pl.when(me < n - 1)
        def _():
            pass_on(1, at).wait_recv()
            part[at] += recvbuf[1, at].astype(jnp.float32)

        outbuf[i] = part[at].astype(outbuf.dtype)
        out_to_sibling(i, core).start()
        out_copy(i).start()

    for a in range(2):
        for j in range(1, WINDOW):
            @pl.when(c + j < spans)
            def _():
                for d in range(seqs):
                    kv_copy(j, d, a).wait_send()
        for d in range(1, seqs):
            kv_copy(0, d, a).wait_send()
    q_copy(core).wait_send()
    for d in range(1, seqs):
        clip_copy(d, s).wait_send()

    def sent(i, carry):
        @pl.when(i // pieces != me)
        def _():
            pass_on(0, i).wait_send()

        return carry

    lax.fori_loop(0, steps, sent, 0)
    for i in range(att_parts):
        att_copy(i, core).wait_send()
    for i in range(pieces):
        out_copy(i).wait()
        out_to_sibling(i, core).wait_send()
        out_to_sibling(i, 1 - core).wait_recv()


def on_device(queries, keys, values, clip_ids, block_mask, out_weight):
    spans = lax.axis_size("span")
    seqs = lax.axis_size("seq")
    n = lax.axis_size("mp")
    _, rows, local_width = queries.shape
    assert GROUP % (local_width // HEAD_DIM // 2) == 0
    depth, out_width = out_weight.shape
    chunk = out_width // n
    width = HEAD_DIM
    pieces = chunk // 2 // width
    bf16 = jnp.bfloat16
    hbm = pl.BlockSpec(memory_space=pl.ANY)
    return pl.pallas_call(
        functools.partial(kernel, spans, seqs, n, pieces),
        out_shape=jax.ShapeDtypeStruct((1, rows, chunk), bf16),
        in_specs=[hbm] * 6,
        out_specs=hbm,
        scratch_shapes=[
            pltpu.VMEM((2, rows, local_width // 2), bf16),
            pltpu.VMEM((rows, local_width // 2), bf16),
            pltpu.VMEM((WINDOW, seqs, rows, HEAD_DIM), bf16),
            pltpu.VMEM((WINDOW, seqs, rows, HEAD_DIM), bf16),
            pltpu.VMEM((2, rows, HEAD_DIM), bf16),
            pltpu.VMEM((1, rows), jnp.int32),
            pltpu.SMEM(block_mask.shape, jnp.int32),
            pltpu.VMEM((seqs, 8, rows), jnp.int32),
            pltpu.VMEM((n * pieces, depth, width), bf16),
            pltpu.VMEM((2, 2 * rows, local_width // 2), bf16),
            pltpu.VMEM((n * pieces, 2 * rows, width), jnp.float32),
            pltpu.VMEM((n * pieces, 2 * rows, width), bf16),
            pltpu.VMEM((2, n * pieces, 2 * rows, width), bf16),
            pltpu.VMEM((pieces, 2 * rows, width), bf16),
            pltpu.SemaphoreType.DMA((8,)),
            pltpu.SemaphoreType.DMA((n * pieces,)),
            pltpu.SemaphoreType.DMA((2,)),
            pltpu.SemaphoreType.DMA((WINDOW, seqs, 2)),
            pltpu.SemaphoreType.DMA((WINDOW, seqs, 2)),
            pltpu.SemaphoreType.DMA((seqs,)),
            pltpu.SemaphoreType.DMA((seqs,)),
            pltpu.SemaphoreType.DMA((n * pieces,)),
            pltpu.SemaphoreType.DMA((2, n * pieces)),
            pltpu.SemaphoreType.DMA((pieces,)),
            pltpu.SemaphoreType.DMA((2,)),
            pltpu.SemaphoreType.DMA((2,)),
            pltpu.SemaphoreType.DMA((pieces,)),
            pltpu.SemaphoreType.DMA((pieces,)),
        ],
        compiler_params=pltpu.CompilerParams(
            collective_id=0, has_side_effects=True, vmem_limit_bytes=64 * 1024 * 1024
        ),
    )(queries, keys, values, clip_ids.reshape(1, rows), block_mask, out_weight)


def solution(mesh):
    in_specs = (
        P("span", "seq", "mp"),
        P("span", "seq", None),
        P("span", "seq", None),
        P("seq"),
        P(),
        P("mp", None),
    )
    out_specs = P("span", "seq", "mp")
    return jax.shard_map(
        on_device, mesh=mesh, in_specs=in_specs, out_specs=out_specs, check_vma=False
    )
```
